32 devices in a mesh: dp: 8 (over z, x), seq: 4 (over y, core).
Axes of the slice: x: 2, y: 2, z: 4, core: 2. Of those that a mesh axis runs over, the one named last changes fastest.
Arguments:
- tokens: bfloat16 [16, 1024, 1024], P('dp', 'seq'), may hold values from -6 to 6
- segments: int32 [16, 1024], P('dp', 'seq'), may hold values from 0 to 4, as said below
- norm_in_gain: bfloat16 [1024], P(('dp', 'seq')), may hold values from 0.5 to 1.5
- gate_in_weight: bfloat16 [1024, 1536], P(('dp', 'seq')), may hold values from -0.1875 to 0.1875
- signal_in_weight: bfloat16 [1024, 1536], P(('dp', 'seq')), may hold values from -0.1875 to 0.1875
- conv_weight: bfloat16 [4, 1536], P(None, ('dp', 'seq')), may hold values from -3 to 3
- rec_gate_weight: bfloat16 [1536, 128], P(('dp', 'seq')), may hold values from -0.5 to 0.5
- input_gate_weight: bfloat16 [1536, 128], P(('dp', 'seq')), may hold values from -0.5 to 0.5
- decay_param: bfloat16 [1536], P(('dp', 'seq')), may hold values from 4 to 16
- branch_out_weight: bfloat16 [1536, 1024], P(('dp', 'seq')), may hold values from -0.4375 to 0.4375
- norm_mid_gain: bfloat16 [1024], P(('dp', 'seq')), may hold values from 0.5 to 1.5
- mlp_gate_weight: bfloat16 [1024, 3072], P(('dp', 'seq')), may hold values from -0.1875 to 0.1875
- mlp_up_weight: bfloat16 [1024, 3072], P(('dp', 'seq')), may hold values from -0.1875 to 0.1875
- mlp_down_weight: bfloat16 [3072, 1024], P(('dp', 'seq')), may hold values from -0.21875 to 0.21875
- cotangent: bfloat16 [16, 1024, 1024], P('dp', 'seq'), may hold values from -6 to 6
Outputs:
- block_out: float32 [16, 1024, 1024], P('dp', 'seq')
- tokens_grad: float32 [16, 1024, 1024], P('dp', 'seq')
- norm_in_grad: float32 [1024], P(('dp', 'seq'))
- gate_in_grad: float32 [1024, 1536], P(('dp', 'seq'))
- signal_in_grad: float32 [1024, 1536], P(('dp', 'seq'))
- conv_weight_grad: float32 [4, 1536], P(None, ('dp', 'seq'))
- rec_gate_grad: float32 [1536, 128], P(('dp', 'seq'))
- input_gate_grad: float32 [1536, 128], P(('dp', 'seq'))
- decay_param_grad: float32 [1536], P(('dp', 'seq'))
- branch_out_grad: float32 [1536, 1024], P(('dp', 'seq'))
- norm_mid_grad: float32 [1024], P(('dp', 'seq'))
- mlp_gate_grad: float32 [1024, 3072], P(('dp', 'seq'))
- mlp_up_grad: float32 [1024, 3072], P(('dp', 'seq'))
- mlp_down_grad: float32 [3072, 1024], P(('dp', 'seq'))
The draws below stay inside these ranges and needn't reach their ends.
Inputs may be any that keep to these rules, and one draw needn't show every extreme that they name: `segments`: within each row the ids start at 0, never fall and rise by one at each new document; every row holds five documents, the third of which begins within the row's first 256 tokens and ends within its last 256 tokens.
All inputs are finite; a program needn't handle non-finite values.
Results may differ from the reference program's by a relative error of at most 0.01.
Values may be sent and summed in bfloat16 or wider, within the bound.
No kernel may reach another device: no remote copies, remote signals or barrier semaphores. Data moves between devices by JAX's collectives and lax.ppermute only.
A program may use at most 320 MiB of HBM per device.

```python
import jax
import jax.numpy as jnp
from jax import lax

D = 1024
LRU = 1536
FF = 3072
BW = 128
CW = 4
ROW_DEV = 256
ROWS = 16
LEN = 1024


def draw_segments(key, part):
    key = jax.random.fold_in(key, 11)
    key_list = jax.random.split(key, 4)
    half_row = ROW_DEV // 2
    early_at = jax.random.randint(key_list[0], (ROWS, 1), 1, half_row)
    begin_at = jax.random.randint(key_list[1], (ROWS, 1), half_row, ROW_DEV)
    finish_at = jax.random.randint(key_list[2], (ROWS, 1), LEN - ROW_DEV + 1, LEN - half_row)
    late_at = jax.random.randint(key_list[3], (ROWS, 1), LEN - half_row, LEN)
    places = jnp.arange(LEN, dtype=jnp.int32)[None, :]
    boundary = (places == early_at) | (places == begin_at) | (places == finish_at) | (places == late_at)
    return jnp.cumsum(boundary.astype(jnp.int32), axis=1).astype(jnp.int32)


def draw_decay_param(key, part):
    key = jax.random.fold_in(key, 5)
    key_list = jax.random.split(key, 3)
    slow_share = 0.5
    choose_slow = jax.random.uniform(key_list[0], (LRU,)) < slow_share
    slow_rate = jnp.exp(jax.random.uniform(key_list[1], (LRU,), minval=jnp.log(0.03 / LEN), maxval=jnp.log(0.11 / LEN)))
    fast_rate = jnp.exp(jax.random.uniform(key_list[2], (LRU,), minval=jnp.log(0.004), maxval=jnp.log(0.008)))
    channel_rate = jnp.where(choose_slow, slow_rate, fast_rate)
    return (-jnp.log(jnp.expm1(channel_rate))).astype(jnp.float32).astype(jnp.bfloat16)


def shard_levels(key, extent, shards, least, top_value):
    factor_of, own = 1.0, jax.random.fold_in(key, 6)
    for position, parts in shards:
        draws = jnp.exp(jax.random.uniform(jax.random.fold_in(own, position), (parts,), jnp.float32, least / len(shards), top_value / len(shards)))
        factor_of = factor_of * jnp.repeat(draws, extent[position] // parts).reshape([-1 if axis == position else 1 for axis in range(len(extent))])
    return factor_of


def noise(stream_key, extent, deviation, most, cuts=(), kind=jnp.bfloat16):
    factor_of = shard_levels(stream_key, extent, cuts, -0.22, 0.18) if cuts else 1.0
    entries = jax.random.normal(stream_key, extent, jnp.float32) * deviation * factor_of
    return jnp.minimum(jnp.maximum(entries, -most), most).astype(kind)


def setup_inputs(seed: int = 0) -> dict:
    keys = jax.random.split(jax.random.key(seed), 16)
    tokens = noise(keys[0], (ROWS, LEN, D), 1.0, 6.0, ((0, 8), (1, 4)))
    segments = draw_segments(jax.random.fold_in(keys[15], 71), 0)
    norm_in_gain = jnp.clip(1.0 + 0.1 * jax.random.normal(keys[2], (D,), jnp.float32), 0.5, 1.5).astype(jnp.bfloat16)
    gate_in_weight = noise(keys[3], (D, LRU), D ** -0.5, 0.1875, ((0, 32),))
    signal_in_weight = noise(keys[4], (D, LRU), D ** -0.5, 0.1875, ((0, 32),))
    conv_weight = noise(keys[5], (CW, LRU), CW ** -0.5, 3.0, ((1, 32),))
    rec_gate_weight = noise(keys[6], (LRU, BW), BW ** -0.5, 0.5, ((0, 32),))
    input_gate_weight = noise(keys[7], (LRU, BW), BW ** -0.5, 0.5, ((0, 32),))
    decay_param = draw_decay_param(jax.random.fold_in(keys[15], 71), 0)
    branch_out_weight = noise(keys[9], (LRU, D), (LRU // 8) ** -0.5, 0.4375, ((0, 32),))
    norm_mid_gain = jnp.clip(1.0 + 0.1 * jax.random.normal(keys[10], (D,), jnp.float32), 0.5, 1.5).astype(jnp.bfloat16)
    mlp_gate_weight = noise(keys[11], (D, FF), D ** -0.5, 0.1875, ((0, 32),))
    mlp_up_weight = noise(keys[12], (D, FF), D ** -0.5, 0.1875, ((0, 32),))
    mlp_down_weight = noise(keys[13], (FF, D), (FF // 4) ** -0.5, 0.21875, ((0, 32),))
    cotangent = noise(keys[14], (ROWS, LEN, D), 1.0, 6.0, ((0, 8), (1, 4)))
    return {"tokens": tokens, "segments": segments, "norm_in_gain": norm_in_gain, "gate_in_weight": gate_in_weight, "signal_in_weight": signal_in_weight, "conv_weight": conv_weight, "rec_gate_weight": rec_gate_weight, "input_gate_weight": input_gate_weight, "decay_param": decay_param, "branch_out_weight": branch_out_weight, "norm_mid_gain": norm_mid_gain, "mlp_gate_weight": mlp_gate_weight, "mlp_up_weight": mlp_up_weight, "mlp_down_weight": mlp_down_weight, "cotangent": cotangent}


epsilon = 1e-06
rate_scale = 8.0
highest = lax.Precision.HIGHEST

@jax.custom_vjp
def low(v):
    return lax.optimization_barrier(v.astype(jnp.bfloat16)).astype(jnp.float32)

@jax.custom_vjp
def low_back(v):
    return v

def low_keep(v):
    return (low(v), None)

def low_pass(kept, grad):
    return (grad,)

def back_keep(v):
    return (v, None)

def back_low(kept, grad):
    return (low(grad),)
low.defvjp(low_keep, low_pass)
low_back.defvjp(back_keep, back_low)

def rms_scale(values, norm_gain):
    return values * lax.rsqrt(lax.optimization_barrier(jnp.mean(values * values, axis=-1, keepdims=True)) + epsilon) * norm_gain

def matmul(left, right):
    return jnp.dot(left, right, precision=highest, preferred_element_type=jnp.float32)

def combine_pairs(earlier, later):
    return (earlier[0] * later[0], later[0] * earlier[1] + later[1])

def block_apply(values, weight):
    row_length = values.shape[0]
    block_width = weight.shape[1]
    blocks = values.reshape(row_length, -1, block_width)
    weight_blocks = weight.reshape(-1, block_width, block_width)
    return jnp.einsum('nhi,hij->nhj', blocks, weight_blocks, precision=highest).reshape(row_length, -1)

def forward_row(inputs, row_ids, norm_in_gain, gate_in_weight, signal_in_weight, conv_weight, rec_gate_weight, input_gate_weight, decay_param, branch_out_weight, norm_mid_gain, mlp_gate_weight, mlp_up_weight, mlp_down_weight):
    normed_in = low(rms_scale(inputs, norm_in_gain))
    gate_pre = low_back(matmul(normed_in, gate_in_weight))
    signal = low_back(low(matmul(normed_in, signal_in_weight)))
    conv_out = conv_weight[0] * signal
    for offset in range(1, conv_weight.shape[0]):
        earlier_signal = jnp.concatenate([jnp.zeros((offset, signal.shape[1]), signal.dtype), signal[:-offset]], axis=0)
        earlier_ids = jnp.concatenate([jnp.full((offset,), -1, jnp.int32), row_ids[:-offset]], axis=0)
        same_mask = (earlier_ids == row_ids).astype(signal.dtype)[:, None]
        conv_out = conv_out + conv_weight[offset] * earlier_signal * same_mask
    conv_low = low(conv_out)
    rec_logit = low_back(block_apply(conv_low, rec_gate_weight))
    input_logit = low_back(block_apply(conv_low, input_gate_weight))
    prev_ids = jnp.concatenate([jnp.full((1,), -1, jnp.int32), row_ids[:-1]], axis=0)
    reset_mask = (prev_ids != row_ids)[:, None]
    log_keep = -rate_scale * jax.nn.softplus(-decay_param) * (0.1 + 0.9 * jax.nn.sigmoid(rec_logit))
    keep_factor = jnp.where(reset_mask, 0.0, jnp.exp(log_keep))
    inject_scale = jnp.where(reset_mask, 1.0, jnp.sqrt(-jnp.expm1(2.0 * log_keep)))
    inject = inject_scale * conv_low * jax.nn.sigmoid(input_logit)
    states = lax.associative_scan(combine_pairs, (keep_factor, inject), axis=0)[1]
    mixed = low(jax.nn.gelu(gate_pre) * states)
    middle = inputs + low_back(matmul(mixed, branch_out_weight))
    normed_mid = low(rms_scale(middle, norm_mid_gain))
    mlp_gate_pre = low_back(matmul(normed_mid, mlp_gate_weight))
    mlp_up_pre = low_back(matmul(normed_mid, mlp_up_weight))
    hidden = low(jax.nn.gelu(mlp_gate_pre) * mlp_up_pre)
    return middle + low_back(matmul(hidden, mlp_down_weight))

def reference(tokens, segments, norm_in_gain, gate_in_weight, signal_in_weight, conv_weight, rec_gate_weight, input_gate_weight, decay_param, branch_out_weight, norm_mid_gain, mlp_gate_weight, mlp_up_weight, mlp_down_weight, cotangent):
    weights = tuple((weight_arg.astype(jnp.float32) for weight_arg in (norm_in_gain, gate_in_weight, signal_in_weight, conv_weight, rec_gate_weight, input_gate_weight, decay_param, branch_out_weight, norm_mid_gain, mlp_gate_weight, mlp_up_weight, mlp_down_weight)))

    def row_step(totals, row_data):
        row_tokens, row_ids, row_cot = row_data

        def forward(inputs_row, *params):
            return forward_row(inputs_row, row_ids, *params)
        row_out, pull_back = jax.vjp(forward, row_tokens.astype(jnp.float32), *weights)
        row_grads = pull_back(row_cot.astype(jnp.float32))
        new_totals = tuple((running + part_grad for running, part_grad in zip(totals, row_grads[1:])))
        return (new_totals, (row_out, row_grads[0]))
    start_totals = tuple((jnp.zeros_like(weight_arg) for weight_arg in weights))
    totals, (outputs, input_grads) = lax.scan(row_step, start_totals, (tokens, segments, cotangent))
    return (outputs, input_grads, totals[0], totals[1], totals[2], totals[3], totals[4], totals[5], totals[6], totals[7], totals[8], totals[9], totals[10], totals[11])
```

```python
import functools

import jax
import jax.numpy as jnp
from jax import lax
from jax.experimental import pallas as pl
from jax.experimental.pallas import tpu as pltpu
from jax.sharding import PartitionSpec as P

epsilon = 1e-06
rate_scale = 8.0
f32 = jnp.float32
bf16 = jnp.bfloat16
gelu_rate = 0.7978845608028654
gelu_cube = 0.044715
halo = 8
vmem_bytes = 48 * 1024 * 1024


def grid_axes():
    dp, seq = lax.axis_size("dp"), lax.axis_size("seq")
    return {
        "z": ("dp", dp, 2, dp // 2),
        "x": ("dp", dp, 1, 2),
        "y": ("seq", seq, 2, seq // 2),
        "c": ("seq", seq, 1, 2),
    }


def place_on(which):
    name, _, stride, count = grid_axes()[which]
    return lax.rem(lax.div(lax.axis_index(name), stride), count)


def ring_step(block, which):
    name, total, stride, count = grid_axes()[which]
    route = []
    for i in range(total):
        k = (i // stride) % count
        route.append((i, i + ((k + 1) % count - k) * stride))
    return lax.ppermute(block, name, route)


def swap_cores(block):
    return ring_step(block, "c")


def passed_along(block, axis, distance):
    devices = range(lax.axis_size(axis))
    route = [(i - distance, i) for i in devices if i - distance in devices]
    return lax.ppermute(block, axis, route)


def gather_rings(piece, order):
    have = []
    for which in order:
        count = grid_axes()[which][3]
        me = place_on(which)
        spot = sum(1 for other in have if "zxyc".index(other) < "zxyc".index(which))
        parts = [piece]
        for _ in range(count - 1):
            parts.append(ring_step(parts[-1], which))
        if count == 2:
            first = me == 0
            a, b = parts
            piece = jnp.stack([jnp.where(first, a, b), jnp.where(first, b, a)], axis=spot)
        else:
            stacked = jnp.zeros(piece.shape[:spot] + (count,) + piece.shape[spot:], piece.dtype)
            for t, part in enumerate(parts):
                stacked = lax.dynamic_update_index_in_dim(
                    stacked, part, lax.rem(me - t + count, count), spot
                )
            piece = stacked
        have.append(which)
    return piece


def scatter_rings(whole, order, left):
    left = list(left)
    wide = whole.dtype
    for which in order:
        count = grid_axes()[which][3]
        me = place_on(which)
        spot = left.index(which)

        def own(back):
            return lax.dynamic_index_in_dim(whole, lax.rem(me - back + count, count), spot, False)

        total = own(1)
        for step in range(count - 1):
            moved = ring_step(total.astype(wide), which)
            total = moved.astype(f32) + own(step + 2).astype(f32)
        left.remove(which)
        whole = total if which == order[-1] else total.astype(wide)
    return whole


def rms_scale(values, norm_gain):
    return (
        values * lax.rsqrt(jnp.mean(values * values, axis=-1, keepdims=True) + epsilon) * norm_gain
    )


def gelu_parts(v):
    th = jnp.tanh(gelu_rate * (v + gelu_cube * v * v * v))
    value = 0.5 * v * (1.0 + th)
    slope = 0.5 * (1.0 + th) + 0.5 * v * (1.0 - th * th) * gelu_rate * (
        1.0 + 3.0 * gelu_cube * v * v
    )
    return value, slope


def scan_rows(a, b, reverse):
    count = a.shape[0]
    row = lax.broadcasted_iota(jnp.int32, a.shape, 0)
    s = 1
    while s < count:
        if s < 8:
            shift = count - s if reverse else s
            valid = row < count - s if reverse else row >= s
            a_far = pltpu.roll(a, shift, 0)
            b_far = pltpu.roll(b, shift, 0)
            b = jnp.where(valid, a * b_far + b, b)
            a = jnp.where(valid, a * a_far, a)
        elif reverse:
            b = jnp.concatenate([a[:-s] * b[s:] + b[:-s], b[-s:]], axis=0)
            a = jnp.concatenate([a[:-s] * a[s:], a[-s:]], axis=0)
        else:
            b = jnp.concatenate([b[:s], a[s:] * b[:-s] + b[s:]], axis=0)
            a = jnp.concatenate([a[:s], a[s:] * a[:-s]], axis=0)
        s *= 2
    return a, b


def minus_expm1(x):
    t = 1.0 + x * (1.0 / 8.0)
    for k in (7.0, 6.0, 5.0, 4.0, 3.0, 2.0):
        t = 1.0 + x * (1.0 / k) * t
    return jnp.where(x > -0.4, -x * t, 1.0 - jnp.exp(x))


def gate_values(conv_low, rec_w, inp_w, rate, reset):
    r = jax.nn.sigmoid(jnp.dot(conv_low, rec_w, preferred_element_type=f32))
    g = jax.nn.sigmoid(jnp.dot(conv_low, inp_w, preferred_element_type=f32))
    log_keep = rate * (0.1 + 0.9 * r)
    keep = jnp.where(reset, 0.0, jnp.exp(log_keep))
    lost = minus_expm1(2.0 * log_keep)
    inverse = lax.rsqrt(lost)
    scale = jnp.where(reset, 1.0, lost * inverse)
    return r, g, keep, lost, inverse, scale


def forward_kernel(
    row_count,
    sig_ref,
    tail_ref,
    mask_ref,
    taps_ref,
    rate_ref,
    rec_ref,
    inp_ref,
    conv_ref,
    keep_ref,
    cum_ref,
    local_ref,
):
    row_tokens = sig_ref.shape[0] // row_count
    for b in range(row_count):
        rows = pl.ds(b * row_tokens, row_tokens)
        sig = sig_ref[rows, :].astype(f32)
        ext = jnp.concatenate([tail_ref[pl.ds(b * halo, halo), :], sig], axis=0)
        conv = taps_ref[0:1, :] * sig
        for k in range(1, taps_ref.shape[0]):
            conv += taps_ref[k : k + 1, :] * pltpu.roll(ext, k, 0)[halo:] * mask_ref[k - 1, rows, :]
        conv_low = conv.astype(bf16)
        conv_ref[rows, :] = conv_low
        reset = mask_ref[0, rows, :] == 0.0
        _, g, keep, _, _, scale = gate_values(
            conv_low, rec_ref[...], inp_ref[...], rate_ref[...], reset
        )
        keep_ref[rows, :] = keep
        cum, local = scan_rows(keep, scale * conv_low.astype(f32) * g, False)
        cum_ref[rows, :] = cum
        local_ref[rows, :] = local


def reverse_kernel(
    row_count, mixed_grad_ref, states_ref, gate_ref, keep_ref, gate_low_ref, tail_ref, local_ref
):
    row_tokens = keep_ref.shape[0] // row_count
    for b in range(row_count):
        rows = pl.ds(b * row_tokens, row_tokens)
        value, slope = gelu_parts(gate_ref[rows, :])
        grad = mixed_grad_ref[rows, :]
        gate_low_ref[rows, :] = (grad * states_ref[rows, :] * slope).astype(bf16)
        keep = keep_ref[rows, :]
        row = lax.broadcasted_iota(jnp.int32, keep.shape, 0)
        next_keep = jnp.where(row == row_tokens - 1, 1.0, pltpu.roll(keep, row_tokens - 1, 0))
        tail, local = scan_rows(next_keep, grad * value, True)
        tail_ref[rows, :] = tail
        local_ref[rows, :] = local


def backward_kernel(
    row_count,
    sig_ref,
    before_ref,
    mask_ref,
    taps_ref,
    rate_ref,
    rec_ref,
    inp_ref,
    conv_ref,
    states_ref,
    state_in_ref,
    tail_ref,
    local_ref,
    grad_in_ref,
    signal_ref,
    head_ref,
    rec_grad_ref,
    inp_grad_ref,
    sums_ref,
):
    row_tokens = sig_ref.shape[0] // row_count
    tap_count = taps_ref.shape[0]
    rate = rate_ref[...]
    sums = [0.0] * (tap_count + 1)
    rec_total = 0.0
    inp_total = 0.0
    for b in range(row_count):
        rows = pl.ds(b * row_tokens, row_tokens)
        conv_low = conv_ref[rows, :]
        conv = conv_low.astype(f32)
        reset = mask_ref[0, rows, :] == 0.0
        r, g, keep, lost, inverse, scale = gate_values(
            conv_low, rec_ref[...], inp_ref[...], rate, reset
        )
        state_grad = local_ref[rows, :] + tail_ref[rows, :] * grad_in_ref[b : b + 1, :]
        states = states_ref[rows, :]
        row = lax.broadcasted_iota(jnp.int32, states.shape, 0)
        before = jnp.where(row == 0, state_in_ref[b : b + 1, :], pltpu.roll(states, 1, 0))
        direct = state_grad * g
        dlog = state_grad * before * keep - jnp.where(
            reset, 0.0, direct * conv * (1.0 - lost) * inverse
        )
        rec_low = (dlog * rate * 0.9 * r * (1.0 - r)).astype(bf16)
        input_low = (direct * scale * conv * (1.0 - g)).astype(bf16)
        sums[0] += jnp.sum(dlog * (0.1 + 0.9 * r), axis=0, keepdims=True)
        first = (((0,), (0,)), ((), ()))
        second = (((1,), (1,)), ((), ()))
        rec_total += lax.dot_general(conv_low, rec_low, first, preferred_element_type=f32)
        inp_total += lax.dot_general(conv_low, input_low, first, preferred_element_type=f32)
        conv_grad = (
            direct * scale
            + lax.dot_general(rec_low, rec_ref[...], second, preferred_element_type=f32)
            + lax.dot_general(input_low, inp_ref[...], second, preferred_element_type=f32)
        )
        sig = sig_ref[rows, :].astype(f32)
        ext = jnp.concatenate([before_ref[pl.ds(b * halo, halo), :], sig], axis=0)
        blank = jnp.zeros((halo, sig.shape[1]), f32)
        back = jnp.concatenate([blank, conv_grad * taps_ref[0:1, :]], axis=0)
        sums[1] += jnp.sum(conv_grad * sig, axis=0, keepdims=True)
        for k in range(1, tap_count):
            part = conv_grad * mask_ref[k - 1, rows, :]
            sums[1 + k] += jnp.sum(part * pltpu.roll(ext, k, 0)[halo:], axis=0, keepdims=True)
            moved = jnp.concatenate([blank, part * taps_ref[k : k + 1, :]], axis=0)
            back += pltpu.roll(moved, row_tokens + halo - k, 0)
        head_ref[pl.ds(b * halo, halo), :] = back[:halo]
        signal_ref[rows, :] = back[halo:]
    rec_grad_ref[...] = rec_total
    inp_grad_ref[...] = inp_total
    for k in range(tap_count + 1):
        sums_ref[k : k + 1, :] = sums[k]


def channel_call(kernel, row_count, ins, outs, width, block, flops):
    def spec(shape):
        if len(shape) == 3:
            return pl.BlockSpec((shape[0], shape[1], block), lambda h: (0, 0, 0))
        if shape == (width, block):
            return pl.BlockSpec((block, block), lambda h: (h, 0))
        return pl.BlockSpec((shape[0], block), lambda h: (0, h))

    moved = sum(a.size * a.dtype.itemsize for a in ins) + sum(
        o.size * o.dtype.itemsize for o in outs
    )
    return pl.pallas_call(
        functools.partial(kernel, row_count),
        grid=(width // block,),
        in_specs=[spec(a.shape) for a in ins],
        out_specs=[spec(o.shape) for o in outs],
        out_shape=outs,
        compiler_params=pltpu.CompilerParams(vmem_limit_bytes=vmem_bytes),
        cost_estimate=pl.CostEstimate(flops=flops, bytes_accessed=moved, transcendentals=0),
    )(*ins)


def carry_before(factor, value, reverse):
    count = lax.axis_size("seq")
    place = lax.axis_index("seq")
    both = lax.all_gather(jnp.stack([factor, value]), "seq")
    state = jnp.zeros_like(value)
    turns = range(count - 1, 0, -1) if reverse else range(count - 1)
    for source in turns:
        passed = place < source if reverse else source < place
        state = jnp.where(passed, both[source, 0] * state + both[source, 1], state)
    return state


def body(
    tokens,
    segments,
    norm_in_gain,
    gate_in_weight,
    signal_in_weight,
    conv_weight,
    rec_gate_weight,
    input_gate_weight,
    decay_param,
    branch_out_weight,
    norm_mid_gain,
    mlp_gate_weight,
    mlp_up_weight,
    mlp_down_weight,
    cotangent,
):
    row_count, row_tokens, model_width = tokens.shape
    lru_width = signal_in_weight.shape[1]
    block_width = rec_gate_weight.shape[1]
    ff_width = mlp_gate_weight.shape[1]
    tap_count = conv_weight.shape[0]
    halo_rows = tap_count - 1
    token_count = row_count * row_tokens
    device_count = lax.axis_size("dp") * lax.axis_size("seq")
    core = place_on("c")
    model_piece = norm_in_gain.shape[0]
    lru_piece = decay_param.shape[0]

    small = jnp.concatenate(
        [norm_in_gain, norm_mid_gain, decay_param, conv_weight.reshape(-1)], axis=0
    )
    small_size = small.shape[0]
    pair_width = 2 * block_width
    small_rows = -(-small_size // pair_width)
    small = jnp.pad(small, (0, small_rows * pair_width - small_size)).reshape(
        small_rows, pair_width
    )
    gate_pair = jnp.concatenate([rec_gate_weight, input_gate_weight], axis=1)
    pack = jnp.concatenate([gate_pair, small], axis=0)
    pack_rows = pack.shape[0]
    pack = jnp.pad(pack, ((0, -pack_rows % 16), (0, 0)))

    full_signal = gather_rings(signal_in_weight, "zyxc").reshape(model_width, lru_width)
    full_gate_in = gather_rings(gate_in_weight, "zxyc").reshape(model_width, lru_width)
    full_pack = gather_rings(pack, "zyxc").reshape(device_count, pack.shape[0], pair_width)
    full_branch = gather_rings(branch_out_weight, "zyxc").reshape(lru_width, model_width)
    full_mlp_gate = gather_rings(mlp_gate_weight, "zyxc").reshape(model_width, ff_width)
    full_mlp_up = gather_rings(mlp_up_weight, "zxyc").reshape(model_width, ff_width)
    full_mlp_down = gather_rings(mlp_down_weight, "xyzc").reshape(ff_width, model_width)

    gate_pairs = full_pack[:, :lru_piece].reshape(lru_width, pair_width)
    full_rec, full_input = gate_pairs[:, :block_width], gate_pairs[:, block_width:]
    smalls = full_pack[:, lru_piece : lru_piece + small_rows].reshape(device_count, -1).astype(f32)
    gain_in = smalls[:, :model_piece].reshape(model_width)
    gain_mid = smalls[:, model_piece : 2 * model_piece].reshape(model_width)
    start = 2 * model_piece
    decay_full = smalls[:, start : start + lru_piece].reshape(lru_width)
    start += lru_piece
    taps = (
        smalls[:, start : start + tap_count * lru_piece]
        .reshape(device_count, tap_count, lru_piece)
        .transpose(1, 0, 2)
        .reshape(tap_count, lru_width)
    )
    rate = (-rate_scale * jax.nn.softplus(-decay_full))[None, :]

    inputs = tokens.astype(f32).reshape(token_count, model_width)
    scale_in = lax.rsqrt(jnp.mean(inputs * inputs, axis=-1, keepdims=True) + epsilon)
    normed_in = (inputs * scale_in * gain_in).astype(bf16)
    signal = jnp.dot(normed_in, full_signal, preferred_element_type=f32).astype(bf16)
    gate_pre = jnp.dot(normed_in, full_gate_in, preferred_element_type=f32)
    tail_ids = passed_along(segments[:, row_tokens - halo_rows :], "seq", 1)
    tail_ids = jnp.where(lax.axis_index("seq") == 0, jnp.int32(-1), tail_ids)
    ids_ext = jnp.concatenate([tail_ids, segments], axis=1)
    masks = jnp.stack(
        [
            (ids_ext[:, halo_rows - k : halo_rows - k + row_tokens] == segments).astype(f32)
            for k in range(1, tap_count)
        ]
    )
    masks = jnp.broadcast_to(
        masks.reshape(halo_rows, token_count, 1), (halo_rows, token_count, block_width)
    )
    tail_signal = passed_along(
        signal.reshape(row_count, row_tokens, lru_width)[:, row_tokens - halo_rows :], "seq", 1
    )
    before = jnp.pad(
        tail_signal.astype(f32), ((0, 0), (halo - halo_rows, 0), (0, 0))
    ).reshape(row_count * halo, lru_width)

    wide_f32 = jax.ShapeDtypeStruct((token_count, lru_width), f32)
    wide_bf16 = jax.ShapeDtypeStruct((token_count, lru_width), bf16)
    block_flops = 4 * token_count * lru_width * block_width
    conv_low, keep, cum_keep, local_state = channel_call(
        forward_kernel,
        row_count,
        [signal, before, masks, taps, rate, full_rec, full_input],
        [wide_bf16, wide_f32, wide_f32, wide_f32],
        lru_width,
        block_width,
        block_flops,
    )
    cum3 = cum_keep.reshape(row_count, row_tokens, lru_width)
    local3 = local_state.reshape(row_count, row_tokens, lru_width)
    state_in = carry_before(cum3[:, -1], local3[:, -1], False)
    states = (local3 + cum3 * state_in[:, None, :]).reshape(token_count, lru_width)
    mixed = (gelu_parts(gate_pre)[0] * states).astype(bf16)
    middle = inputs + jnp.dot(mixed, full_branch, preferred_element_type=f32)
    scale_mid = lax.rsqrt(jnp.mean(middle * middle, axis=-1, keepdims=True) + epsilon)
    normed_mid = (middle * scale_mid * gain_mid).astype(bf16)
    mlp_gate_pre = jnp.dot(normed_mid, full_mlp_gate, preferred_element_type=f32)
    mlp_up_pre = jnp.dot(normed_mid, full_mlp_up, preferred_element_type=f32)
    mlp_act, mlp_slope = gelu_parts(mlp_gate_pre)
    hidden = (mlp_act * mlp_up_pre).astype(bf16)
    block_out = middle + jnp.dot(hidden, full_mlp_down, preferred_element_type=f32)

    out_grad = cotangent.reshape(token_count, model_width)

    def other_half(a):
        width = a.shape[1] // 2
        return lax.dynamic_slice_in_dim(a, (1 - core) * width, width, 1)

    def my_half(a):
        width = a.shape[1] // 2
        return lax.dynamic_slice_in_dim(a, core * width, width, 1)

    def both_rows(a):
        return jnp.concatenate([a, swap_cores(a)], axis=0)

    def both_halves(a):
        return jnp.concatenate([my_half(a), swap_cores(other_half(a))], axis=0)

    def chip_grad(left_rows, right_half, order):
        whole = lax.dot_general(
            left_rows, right_half, (((0,), (0,)), ((), ())), preferred_element_type=f32
        ).astype(bf16)
        return chip_scatter(whole, order)

    def chip_scatter(whole, order):
        sizes = [grid_axes()[a][3] for a in "zxy"]
        rows = whole.shape[0] // (sizes[0] * sizes[1] * sizes[2])
        mine = scatter_rings(whole.reshape(*sizes, rows, whole.shape[1]), order, "zxy")
        mine = mine.reshape(2, rows // 2, whole.shape[1])
        sent = swap_cores(lax.dynamic_index_in_dim(mine, 1 - core, 0, False))
        kept = lax.dynamic_index_in_dim(mine, core, 0, False)
        first = core == 0
        return jnp.concatenate(
            [jnp.where(first, kept, sent), jnp.where(first, sent, kept)], axis=1
        )

    down_shard = chip_grad(both_rows(hidden), both_halves(out_grad), "zyx")
    hidden_grad = lax.dot_general(
        out_grad, full_mlp_down, (((1,), (1,)), ((), ())), preferred_element_type=f32
    )
    gate_grad_low = (hidden_grad * mlp_up_pre * mlp_slope).astype(bf16)
    up_grad_low = (hidden_grad * mlp_act).astype(bf16)
    normed_mid_pair = both_rows(normed_mid)
    mlp_gate_shard = chip_grad(normed_mid_pair, both_halves(gate_grad_low), "xyz")
    mlp_up_shard = chip_grad(normed_mid_pair, both_halves(up_grad_low), "yxz")
    transposed = (((1,), (1,)), ((), ()))
    normed_mid_grad = lax.dot_general(
        gate_grad_low, full_mlp_gate, transposed, preferred_element_type=f32
    ) + lax.dot_general(up_grad_low, full_mlp_up, transposed, preferred_element_type=f32)

    def norm_back(grad, values, scale, gain):
        weighted = grad * gain
        inner = jnp.mean(weighted * values, axis=-1, keepdims=True)
        back = scale * weighted - values * (scale * scale * scale * inner)
        return back, jnp.sum(grad * values * scale, axis=0)

    mid_back, gain_mid_grad = norm_back(normed_mid_grad, middle, scale_mid, gain_mid)
    middle_grad = out_grad.astype(f32) + mid_back
    middle_low = middle_grad.astype(bf16)
    branch_shard = chip_grad(both_rows(mixed), both_halves(middle_low), "xyz")
    mixed_grad = lax.dot_general(middle_low, full_branch, transposed, preferred_element_type=f32)
    gate_pre_low, tail_keep, local_grad = channel_call(
        reverse_kernel,
        row_count,
        [mixed_grad, states, gate_pre, keep],
        [wide_bf16, wide_f32, wide_f32],
        lru_width,
        block_width,
        0,
    )
    normed_in_pair = both_rows(normed_in)
    gate_in_shard = chip_grad(normed_in_pair, both_halves(gate_pre_low), "yxz")
    first_keep = keep.reshape(row_count, row_tokens, lru_width)[:, 0]
    head_factor = first_keep * tail_keep.reshape(row_count, row_tokens, lru_width)[:, 0]
    head_grad = first_keep * local_grad.reshape(row_count, row_tokens, lru_width)[:, 0]
    grad_in = carry_before(head_factor, head_grad, True)
    square = jax.ShapeDtypeStruct((lru_width, block_width), f32)
    signal_part, head_part, rec_full, input_full, sums = channel_call(
        backward_kernel,
        row_count,
        [
            signal,
            before,
            masks,
            taps,
            rate,
            full_rec,
            full_input,
            conv_low,
            states,
            state_in,
            tail_keep,
            local_grad,
            grad_in,
        ],
        [
            wide_f32,
            jax.ShapeDtypeStruct((row_count * halo, lru_width), f32),
            square,
            square,
            jax.ShapeDtypeStruct((tap_count + 1, lru_width), f32),
        ],
        lru_width,
        block_width,
        3 * block_flops,
    )
    from_right = passed_along(
        head_part.reshape(row_count, halo, lru_width)[:, halo - halo_rows :].astype(bf16),
        "seq",
        -1,
    ).astype(f32)
    signal_low = (
        (
            signal_part.reshape(row_count, row_tokens, lru_width)
            + jnp.pad(from_right, ((0, 0), (row_tokens - halo_rows, 0), (0, 0)))
        )
        .astype(bf16)
        .reshape(token_count, lru_width)
    )
    signal_shard = chip_grad(normed_in_pair, both_halves(signal_low), "xyz")
    pair_grads = jnp.where(core == 0, rec_full, input_full) + swap_cores(
        jnp.where(core == 0, input_full, rec_full).astype(bf16)
    ).astype(f32)
    pair_shard = chip_scatter(pair_grads.astype(bf16), "yxz")
    normed_in_grad = lax.dot_general(
        gate_pre_low, full_gate_in, transposed, preferred_element_type=f32
    ) + lax.dot_general(signal_low, full_signal, transposed, preferred_element_type=f32)
    in_back, gain_in_grad = norm_back(normed_in_grad, inputs, scale_in, gain_in)
    tokens_grad = (middle_grad + in_back).reshape(tokens.shape)

    decay_grad = sums[0] * rate_scale * jax.nn.sigmoid(-decay_full)
    tap_grads = sums[1:].reshape(tap_count, device_count, lru_piece).transpose(1, 0, 2)
    small_grads = jnp.concatenate(
        [
            gain_in_grad.reshape(device_count, model_piece),
            gain_mid_grad.reshape(device_count, model_piece),
            decay_grad.reshape(device_count, lru_piece),
            tap_grads.reshape(device_count, tap_count * lru_piece),
        ],
        axis=1,
    )
    sizes = [grid_axes()[a][3] for a in "zxyc"]
    small_shard = scatter_rings(small_grads.reshape(*sizes, 1, small_size), "cxyz", "zxyc")[0]
    start = 2 * model_piece + lru_piece
    return (
        block_out.reshape(tokens.shape),
        tokens_grad,
        small_shard[:model_piece],
        gate_in_shard,
        signal_shard,
        small_shard[start:].reshape(tap_count, lru_piece),
        pair_shard[:, :block_width],
        pair_shard[:, block_width:],
        small_shard[2 * model_piece : start],
        branch_shard,
        small_shard[model_piece : 2 * model_piece],
        mlp_gate_shard,
        mlp_up_shard,
        down_shard,
    )


def solution(mesh):
    rows = P(("dp", "seq"))
    matrix = P(("dp", "seq"), None)
    columns = P(None, ("dp", "seq"))
    tokens = P("dp", "seq", None)
    return jax.shard_map(
        body,
        mesh=mesh,
        in_specs=(
            tokens,
            P("dp", "seq"),
            rows,
            matrix,
            matrix,
            columns,
            matrix,
            matrix,
            rows,
            matrix,
            rows,
            matrix,
            matrix,
            matrix,
            tokens,
        ),
        out_specs=(
            tokens,
            tokens,
            rows,
            matrix,
            matrix,
            columns,
            matrix,
            matrix,
            rows,
            matrix,
            rows,
            matrix,
            matrix,
            matrix,
        ),
        check_vma=False,
    )
```

```python
import functools

import jax
import jax.numpy as jnp
from jax import lax
from jax.experimental import pallas as pl
from jax.experimental.pallas import tpu as pltpu
from jax.sharding import PartitionSpec as P

epsilon = 1e-06
rate_scale = 8.0
f32 = jnp.float32
bf16 = jnp.bfloat16
gelu_rate = 0.7978845608028654
gelu_cube = 0.044715
halo = 8
vmem_bytes = 48 * 1024 * 1024


def grid_axes():
    dp, seq = lax.axis_size("dp"), lax.axis_size("seq")
    return {
        "z": ("dp", dp, 2, dp // 2),
        "x": ("dp", dp, 1, 2),
        "y": ("seq", seq, 2, seq // 2),
        "c": ("seq", seq, 1, 2),
    }


def place_on(which):
    name, _, stride, count = grid_axes()[which]
    return lax.rem(lax.div(lax.axis_index(name), stride), count)


def ring_step(block, which):
    name, total, stride, count = grid_axes()[which]
    route = []
    for i in range(total):
        k = (i // stride) % count
        route.append((i, i + ((k + 1) % count - k) * stride))
    return lax.ppermute(block, name, route)


def swap_cores(block):
    return ring_step(block, "c")


def passed_along(block, axis, distance):
    devices = range(lax.axis_size(axis))
    route = [(i - distance, i) for i in devices if i - distance in devices]
    return lax.ppermute(block, axis, route)


def after(value, *others):
    return lax.optimization_barrier((value, *others))[0]


def hop(block, which, distance):
    name, total, stride, count = grid_axes()[which]
    route = []
    for i in range(total):
        k = (i // stride) % count
        route.append((i, i + ((k + distance) % count - k) * stride))
    return lax.ppermute(block, name, route)


class Flight:
    def done(self):
        return not self.order


class Gather(Flight):
    def __init__(self, piece, order):
        self.piece = piece
        self.order = list(order)
        self.have = []

    def sends(self, which):
        return [self.piece] * (grid_axes()[which][3] - 1)

    def finish(self):
        which = self.order.pop(0)
        count = grid_axes()[which][3]
        me = place_on(which)
        spot = sum(1 for other in self.have if "zxyc".index(other) < "zxyc".index(which))
        piece = self.piece
        parts = [piece] + self.moved
        if count == 2:
            first = me == 0
            a, b = parts
            piece = jnp.stack([jnp.where(first, a, b), jnp.where(first, b, a)], axis=spot)
        else:
            stacked = jnp.zeros(piece.shape[:spot] + (count,) + piece.shape[spot:], piece.dtype)
            for t, part in enumerate(parts):
                stacked = lax.dynamic_update_index_in_dim(
                    stacked, part, lax.rem(me - t + count, count), spot
                )
            piece = stacked
        self.have.append(which)
        self.piece = piece


class Scatter(Flight):
    def __init__(self, whole, order, left="zxy"):
        self.whole = whole
        self.wide = whole.dtype
        self.order = list(order)
        self.left = list(left)

    def own(self, ahead):
        which = self.order[0]
        count = grid_axes()[which][3]
        return lax.dynamic_index_in_dim(
            self.whole,
            lax.rem(place_on(which) + ahead, count),
            self.left.index(which),
            False,
        )

    def sends(self, which):
        return [self.own(d) for d in range(1, grid_axes()[which][3])]

    def finish(self):
        total = self.own(0).astype(f32)
        for moved in self.moved:
            total = total + moved.astype(f32)
        self.left.remove(self.order.pop(0))
        self.whole = total.astype(self.wide) if self.order else total


def launch(value, *flights):
    blocks = [f.sends(f.order[0]) for f in flights]
    value, blocks = lax.optimization_barrier((value, blocks))
    for f, sent in zip(flights, blocks):
        which = f.order[0]
        f.moved = [hop(block, which, d + 1) for d, block in enumerate(sent)]
    return value


def land(value, *flights):
    value, landed = lax.optimization_barrier((value, [f.moved for f in flights]))
    for f, moved in zip(flights, landed):
        f.moved = moved
        f.finish()
    return value


def tick(value, *flights):
    value = land(value, *flights)
    return launch(value, *[f for f in flights if not f.done()])


def run_out(flight):
    if not flight.done():
        flight.finish()
    while not flight.done():
        launch(None, flight)
        flight.finish()
    return flight.whole


def gelu_parts(v):
    th = jnp.tanh(gelu_rate * (v + gelu_cube * v * v * v))
    value = 0.5 * v * (1.0 + th)
    slope = 0.5 * (1.0 + th) + 0.5 * v * (1.0 - th * th) * gelu_rate * (
        1.0 + 3.0 * gelu_cube * v * v
    )
    return value, slope


def scan_rows(a, b, reverse):
    count = a.shape[0]
    row = lax.broadcasted_iota(jnp.int32, a.shape, 0)
    s = 1
    while s < count:
        if s < 8:
            shift = count - s if reverse else s
            valid = row < count - s if reverse else row >= s
            a_far = pltpu.roll(a, shift, 0)
            b_far = pltpu.roll(b, shift, 0)
            b = jnp.where(valid, a * b_far + b, b)
            a = jnp.where(valid, a * a_far, a)
        elif reverse:
            b = jnp.concatenate([a[:-s] * b[s:] + b[:-s], b[-s:]], axis=0)
            a = jnp.concatenate([a[:-s] * a[s:], a[-s:]], axis=0)
        else:
            b = jnp.concatenate([b[:s], a[s:] * b[:-s] + b[s:]], axis=0)
            a = jnp.concatenate([a[:s], a[s:] * a[:-s]], axis=0)
        s *= 2
    return a, b


def minus_expm1(x):
    t = 1.0 + x * (1.0 / 8.0)
    for k in (7.0, 6.0, 5.0, 4.0, 3.0, 2.0):
        t = 1.0 + x * (1.0 / k) * t
    return jnp.where(x > -0.4, -x * t, 1.0 - jnp.exp(x))


def gate_values(conv_low, rec_w, inp_w, rate, reset):
    r = jax.nn.sigmoid(jnp.dot(conv_low, rec_w, preferred_element_type=f32))
    g = jax.nn.sigmoid(jnp.dot(conv_low, inp_w, preferred_element_type=f32))
    log_keep = rate * (0.1 + 0.9 * r)
    keep = jnp.where(reset, 0.0, jnp.exp(log_keep))
    lost = minus_expm1(2.0 * log_keep)
    inverse = lax.rsqrt(lost)
    scale = jnp.where(reset, 1.0, lost * inverse)
    return r, g, keep, lost, inverse, scale


def forward_kernel(
    row_count,
    sig_ref,
    tail_ref,
    mask_ref,
    taps_ref,
    rate_ref,
    rec_ref,
    inp_ref,
    conv_ref,
    keep_ref,
    cum_ref,
    local_ref,
):
    row_tokens = sig_ref.shape[0] // row_count
    for b in range(row_count):
        rows = pl.ds(b * row_tokens, row_tokens)
        sig = sig_ref[rows, :].astype(f32)
        ext = jnp.concatenate([tail_ref[pl.ds(b * halo, halo), :], sig], axis=0)
        conv = taps_ref[0:1, :] * sig
        for k in range(1, taps_ref.shape[0]):
            conv += taps_ref[k : k + 1, :] * pltpu.roll(ext, k, 0)[halo:] * mask_ref[k - 1, rows, :]
        conv_low = conv.astype(bf16)
        conv_ref[rows, :] = conv_low
        reset = mask_ref[0, rows, :] == 0.0
        _, g, keep, _, _, scale = gate_values(
            conv_low, rec_ref[...], inp_ref[...], rate_ref[...], reset
        )
        keep_ref[rows, :] = keep
        cum, local = scan_rows(keep, scale * conv_low.astype(f32) * g, False)
        cum_ref[rows, :] = cum
        local_ref[rows, :] = local


def reverse_kernel(
    row_count, mixed_grad_ref, states_ref, gate_ref, keep_ref, gate_low_ref, tail_ref, local_ref
):
    row_tokens = keep_ref.shape[0] // row_count
    for b in range(row_count):
        rows = pl.ds(b * row_tokens, row_tokens)
        value, slope = gelu_parts(gate_ref[rows, :])
        grad = mixed_grad_ref[rows, :]
        gate_low_ref[rows, :] = (grad * states_ref[rows, :] * slope).astype(bf16)
        keep = keep_ref[rows, :]
        row = lax.broadcasted_iota(jnp.int32, keep.shape, 0)
        next_keep = jnp.where(row == row_tokens - 1, 1.0, pltpu.roll(keep, row_tokens - 1, 0))
        tail, local = scan_rows(next_keep, grad * value, True)
        tail_ref[rows, :] = tail
        local_ref[rows, :] = local


def backward_kernel(
    row_count,
    sig_ref,
    before_ref,
    mask_ref,
    taps_ref,
    rate_ref,
    rec_ref,
    inp_ref,
    conv_ref,
    states_ref,
    state_in_ref,
    tail_ref,
    local_ref,
    grad_in_ref,
    signal_ref,
    head_ref,
    rec_grad_ref,
    inp_grad_ref,
    sums_ref,
):
    row_tokens = sig_ref.shape[0] // row_count
    tap_count = taps_ref.shape[0]
    rate = rate_ref[...]
    sums = [0.0] * (tap_count + 1)
    rec_total = 0.0
    inp_total = 0.0
    for b in range(row_count):
        rows = pl.ds(b * row_tokens, row_tokens)
        conv_low = conv_ref[rows, :]
        conv = conv_low.astype(f32)
        reset = mask_ref[0, rows, :] == 0.0
        r, g, keep, lost, inverse, scale = gate_values(
            conv_low, rec_ref[...], inp_ref[...], rate, reset
        )
        state_grad = local_ref[rows, :] + tail_ref[rows, :] * grad_in_ref[b : b + 1, :]
        states = states_ref[rows, :]
        row = lax.broadcasted_iota(jnp.int32, states.shape, 0)
        before = jnp.where(row == 0, state_in_ref[b : b + 1, :], pltpu.roll(states, 1, 0))
        direct = state_grad * g
        dlog = state_grad * before * keep - jnp.where(
            reset, 0.0, direct * conv * (1.0 - lost) * inverse
        )
        rec_low = (dlog * rate * 0.9 * r * (1.0 - r)).astype(bf16)
        input_low = (direct * scale * conv * (1.0 - g)).astype(bf16)
        sums[0] += jnp.sum(dlog * (0.1 + 0.9 * r), axis=0, keepdims=True)
        first = (((0,), (0,)), ((), ()))
        second = (((1,), (1,)), ((), ()))
        rec_total += lax.dot_general(conv_low, rec_low, first, preferred_element_type=f32)
        inp_total += lax.dot_general(conv_low, input_low, first, preferred_element_type=f32)
        conv_grad = (
            direct * scale
            + lax.dot_general(rec_low, rec_ref[...], second, preferred_element_type=f32)
            + lax.dot_general(input_low, inp_ref[...], second, preferred_element_type=f32)
        )
        sig = sig_ref[rows, :].astype(f32)
        ext = jnp.concatenate([before_ref[pl.ds(b * halo, halo), :], sig], axis=0)
        blank = jnp.zeros((halo, sig.shape[1]), f32)
        back = jnp.concatenate([blank, conv_grad * taps_ref[0:1, :]], axis=0)
        sums[1] += jnp.sum(conv_grad * sig, axis=0, keepdims=True)
        for k in range(1, tap_count):
            part = conv_grad * mask_ref[k - 1, rows, :]
            sums[1 + k] += jnp.sum(part * pltpu.roll(ext, k, 0)[halo:], axis=0, keepdims=True)
            moved = jnp.concatenate([blank, part * taps_ref[k : k + 1, :]], axis=0)
            back += pltpu.roll(moved, row_tokens + halo - k, 0)
        head_ref[pl.ds(b * halo, halo), :] = back[:halo]
        signal_ref[rows, :] = back[halo:]
    rec_grad_ref[...] = rec_total
    inp_grad_ref[...] = inp_total
    for k in range(tap_count + 1):
        sums_ref[k : k + 1, :] = sums[k]


def channel_call(kernel, row_count, ins, outs, width, block, flops):
    def spec(shape):
        if len(shape) == 3:
            return pl.BlockSpec((shape[0], shape[1], block), lambda h: (0, 0, 0))
        if shape == (width, block):
            return pl.BlockSpec((block, block), lambda h: (h, 0))
        return pl.BlockSpec((shape[0], block), lambda h: (0, h))

    return pl.pallas_call(
        functools.partial(kernel, row_count),
        grid=(width // block,),
        in_specs=[spec(a.shape) for a in ins],
        out_specs=[spec(o.shape) for o in outs],
        out_shape=outs,
        compiler_params=pltpu.CompilerParams(vmem_limit_bytes=vmem_bytes),
        cost_estimate=pl.CostEstimate(flops=flops, bytes_accessed=1, transcendentals=0),
    )(*ins)


def feature_call(kernel, core, grid, ins, in_specs, outs, out_specs, scratch=()):
    return pl.pallas_call(
        kernel,
        grid_spec=pltpu.PrefetchScalarGridSpec(
            num_scalar_prefetch=1,
            grid=(grid,),
            in_specs=in_specs,
            out_specs=out_specs,
            scratch_shapes=list(scratch),
        ),
        out_shape=outs,
        compiler_params=pltpu.CompilerParams(vmem_limit_bytes=vmem_bytes),
        cost_estimate=pl.CostEstimate(flops=1, bytes_accessed=1, transcendentals=0),
    )(core, *ins)


def whole_spec(shape):
    return pl.BlockSpec(shape, lambda j, core: (0,) * len(shape))


def mlp_kernel(core_ref, normed_ref, gate_w_ref, up_w_ref, act_ref, rise_ref, hidden_ref):
    normed = normed_ref[...]
    gate = jnp.dot(normed, gate_w_ref[...], preferred_element_type=f32)
    up = jnp.dot(normed, up_w_ref[...], preferred_element_type=f32)
    value, slope = gelu_parts(gate)
    act_ref[...] = value
    rise_ref[...] = up * slope
    hidden_ref[...] = (value * up).astype(bf16)


def down_kernel(core_ref, hidden_ref, down_ref, middle_ref, out_ref):
    @pl.when(pl.program_id(0) == 0)
    def _():
        out_ref[...] = middle_ref[...]

    out_ref[...] += jnp.dot(hidden_ref[...], down_ref[...], preferred_element_type=f32)


def hidden_grad_kernel(
    core_ref, grad_ref, down_ref, act_ref, rise_ref, gate_my, gate_other, up_my, up_other
):
    grad = lax.dot_general(
        grad_ref[...], down_ref[...], (((1,), (1,)), ((), ())), preferred_element_type=f32
    )
    gate_low = (grad * rise_ref[...]).astype(bf16)
    up_low = (grad * act_ref[...]).astype(bf16)
    mine = pl.program_id(0) < pl.num_programs(0) // 2

    @pl.when(mine)
    def _():
        gate_my[...] = gate_low
        up_my[...] = up_low

    @pl.when(jnp.logical_not(mine))
    def _():
        gate_other[...] = gate_low
        up_other[...] = up_low


def middle_kernel(
    core_ref,
    gate_my,
    gate_other,
    up_my,
    up_other,
    gate_w_ref,
    up_w_ref,
    middle_ref,
    grad_ref,
    gain_ref,
    middle_grad_ref,
    low_ref,
    low_my,
    low_other,
    gain_grad_ref,
    total,
):
    j = pl.program_id(0)
    transposed = (((1,), (1,)), ((), ()))

    @pl.when(j == 0)
    def _():
        total[...] = jnp.zeros_like(total)

    def add(gate_ref, up_ref):
        total[...] += lax.dot_general(
            gate_ref[...], gate_w_ref[...], transposed, preferred_element_type=f32
        ) + lax.dot_general(up_ref[...], up_w_ref[...], transposed, preferred_element_type=f32)

    mine = j < pl.num_programs(0) // 2

    @pl.when(mine)
    def _():
        add(gate_my, up_my)

    @pl.when(jnp.logical_not(mine))
    def _():
        add(gate_other, up_other)

    @pl.when(j == pl.num_programs(0) - 1)
    def _():
        middle = middle_ref[...]
        scale = lax.rsqrt(jnp.mean(middle * middle, axis=-1, keepdims=True) + epsilon)
        grad = total[...]
        weighted = grad * gain_ref[...]
        inner = jnp.mean(weighted * middle, axis=-1, keepdims=True)
        back = scale * weighted - middle * (scale * scale * scale * inner)
        middle_grad = grad_ref[...].astype(f32) + back
        middle_grad_ref[...] = middle_grad
        low = middle_grad.astype(bf16)
        low_ref[...] = low
        half = low.shape[1] // 2
        first = core_ref[0] == 0

        @pl.when(first)
        def _():
            low_my[...] = low[:, :half]
            low_other[...] = low[:, half:]

        @pl.when(jnp.logical_not(first))
        def _():
            low_my[...] = low[:, half:]
            low_other[...] = low[:, :half]

        gain_grad_ref[...] = jnp.sum(grad * middle * scale, axis=0, keepdims=True)


def carry_before(factor, value, reverse):
    count = lax.axis_size("seq")
    place = lax.axis_index("seq")
    both = lax.all_gather(jnp.stack([factor, value]), "seq")
    state = jnp.zeros_like(value)
    turns = range(count - 1, 0, -1) if reverse else range(count - 1)
    for source in turns:
        passed = place < source if reverse else source < place
        state = jnp.where(passed, both[source, 0] * state + both[source, 1], state)
    return state


def body(
    tokens,
    segments,
    norm_in_gain,
    gate_in_weight,
    signal_in_weight,
    conv_weight,
    rec_gate_weight,
    input_gate_weight,
    decay_param,
    branch_out_weight,
    norm_mid_gain,
    mlp_gate_weight,
    mlp_up_weight,
    mlp_down_weight,
    cotangent,
):
    row_count, row_tokens, model_width = tokens.shape
    lru_width = signal_in_weight.shape[1]
    block_width = rec_gate_weight.shape[1]
    ff_width = mlp_gate_weight.shape[1]
    tap_count = conv_weight.shape[0]
    halo_rows = tap_count - 1
    token_count = row_count * row_tokens
    device_count = lax.axis_size("dp") * lax.axis_size("seq")
    core = place_on("c")
    model_piece = norm_in_gain.shape[0]
    lru_piece = decay_param.shape[0]

    small = jnp.concatenate(
        [
            rec_gate_weight.reshape(-1),
            input_gate_weight.reshape(-1),
            norm_in_gain,
            norm_mid_gain,
            decay_param,
            conv_weight.reshape(-1),
        ]
    )
    pack_width = -(-small.shape[0] // (model_piece * 128)) * 128
    pack = jnp.pad(small, (0, model_piece * pack_width - small.shape[0]))
    pack = pack.reshape(model_piece, pack_width)
    everywhere = ("dp", "seq")
    lru_half = lru_width // 2
    mlp_pair = jnp.concatenate([mlp_gate_weight, mlp_up_weight], axis=1)
    full_mlp = lax.all_gather(mlp_pair, everywhere, axis=0, tiled=True)
    full_mlp_down = lax.all_gather(mlp_down_weight, everywhere, axis=0, tiled=True)
    s1 = Gather(signal_in_weight[:, :lru_half], "zyxc")
    s2 = Gather(jnp.concatenate([signal_in_weight[:, lru_half:], pack], axis=1), "zxyc")
    launch(None, s1, s2)
    tick(None, s1, s2)
    gi = Gather(after(gate_in_weight, s1.piece), "zxyc")
    br = Gather(after(branch_out_weight, s1.piece), "zyxc")
    launch(None, gi, br)
    tick(None, s1, s2)
    tick(None, s1, s2, gi, br)
    land(None, s1, s2)
    smalls = s2.piece.reshape(model_width, -1)
    full_signal = jnp.concatenate(
        [s1.piece.reshape(model_width, -1), smalls[:, :lru_half]], axis=1
    )
    smalls = smalls[:, lru_half:].reshape(device_count, model_piece * pack_width)
    gate_size = lru_piece * block_width
    full_rec = smalls[:, :gate_size].reshape(lru_width, block_width)
    full_input = smalls[:, gate_size : 2 * gate_size].reshape(lru_width, block_width)
    smalls = smalls[:, 2 * gate_size :].astype(f32)
    gain_in = smalls[:, :model_piece].reshape(model_width)
    gain_mid = smalls[:, model_piece : 2 * model_piece].reshape(model_width)
    start = 2 * model_piece
    decay_full = smalls[:, start : start + lru_piece].reshape(lru_width)
    start += lru_piece
    taps = (
        smalls[:, start : start + tap_count * lru_piece]
        .reshape(device_count, tap_count, lru_piece)
        .transpose(1, 0, 2)
        .reshape(tap_count, lru_width)
    )
    rate = (-rate_scale * jax.nn.softplus(-decay_full))[None, :]

    def other_half(a):
        width = a.shape[1] // 2
        return lax.dynamic_slice_in_dim(a, (1 - core) * width, width, 1)

    def my_half(a):
        width = a.shape[1] // 2
        return lax.dynamic_slice_in_dim(a, core * width, width, 1)

    def both_rows(a):
        return jnp.concatenate([a, swap_cores(a)], axis=0)

    def both_halves(a):
        return jnp.concatenate([my_half(a), swap_cores(other_half(a))], axis=0)

    out_grad = cotangent.reshape(token_count, model_width)

    inputs = tokens.astype(f32).reshape(token_count, model_width)
    tail_tokens = passed_along(tokens[:, row_tokens - halo_rows :], "seq", 1)

    def norm_scale(values):
        return lax.rsqrt(jnp.mean(values * values, axis=-1, keepdims=True) + epsilon)

    scale_in = norm_scale(inputs)
    normed_in = (inputs * scale_in * gain_in).astype(bf16)
    tail_rows = jnp.pad(tail_tokens.astype(f32), ((0, 0), (halo - halo_rows, 0), (0, 0)))
    tail_rows = tail_rows.reshape(row_count * halo, model_width)
    tail_normed = (tail_rows * norm_scale(tail_rows) * gain_in).astype(bf16)
    before = (
        jnp.dot(tail_normed, full_signal, preferred_element_type=f32).astype(bf16).astype(f32)
    )
    signal = jnp.dot(normed_in, full_signal, preferred_element_type=f32).astype(bf16)
    tail_ids = passed_along(segments[:, row_tokens - halo_rows :], "seq", 1)
    tail_ids = jnp.where(lax.axis_index("seq") == 0, jnp.int32(-1), tail_ids)
    ids_ext = jnp.concatenate([tail_ids, segments], axis=1)
    masks = jnp.stack(
        [
            (ids_ext[:, halo_rows - k : halo_rows - k + row_tokens] == segments).astype(f32)
            for k in range(1, tap_count)
        ]
    )
    masks = jnp.broadcast_to(
        masks.reshape(halo_rows, token_count, 1), (halo_rows, token_count, block_width)
    )

    wide_f32 = jax.ShapeDtypeStruct((token_count, lru_width), f32)
    wide_bf16 = jax.ShapeDtypeStruct((token_count, lru_width), bf16)
    kernel_flops = 1
    conv_low, keep, cum_keep, local_state = channel_call(
        forward_kernel,
        row_count,
        [signal, before, masks, taps, rate, full_rec, full_input],
        [wide_bf16, wide_f32, wide_f32, wide_f32],
        lru_width,
        block_width,
        kernel_flops,
    )
    cum3 = cum_keep.reshape(row_count, row_tokens, lru_width)
    local3 = local_state.reshape(row_count, row_tokens, lru_width)
    state_in = carry_before(cum3[:, -1], local3[:, -1], False)
    state_in = tick(state_in, gi, br)
    state_in = land(tick(state_in, gi, br), gi, br)
    full_gate_in = gi.piece.reshape(model_width, lru_width)
    gate_pre = jnp.dot(normed_in, full_gate_in, preferred_element_type=f32)
    states = (local3 + cum3 * state_in[:, None, :]).reshape(token_count, lru_width)
    mixed = (gelu_parts(gate_pre)[0] * states).astype(bf16)
    full_branch = br.piece.reshape(lru_width, model_width)
    middle = inputs + jnp.dot(mixed, full_branch, preferred_element_type=f32)
    scale_mid = norm_scale(middle)
    normed_mid = (middle * scale_mid * gain_mid).astype(bf16)
    tile = 512
    tiles = ff_width // tile
    tokens_model = (token_count, model_width)
    tokens_tile = (token_count, tile)
    core_number = core.astype(jnp.int32).reshape(1)

    def turned(j, core):
        return lax.rem(j + core[0] * (tiles // 2), tiles)

    def array(shape, kind):
        return jax.ShapeDtypeStruct(shape, kind)

    plain = pl.BlockSpec(tokens_tile, lambda j, core: (0, j))
    mlp_act, mlp_rise, hidden = feature_call(
        mlp_kernel,
        core_number,
        tiles,
        [normed_mid, full_mlp, full_mlp],
        [
            whole_spec(tokens_model),
            pl.BlockSpec((model_width, tile), lambda j, core: (0, j)),
            pl.BlockSpec((model_width, tile), lambda j, core: (0, j + tiles)),
        ],
        [
            array((token_count, ff_width), f32),
            array((token_count, ff_width), f32),
            array((token_count, ff_width), bf16),
        ],
        [plain, plain, plain],
    )


    def chip_grad(left_rows, right_half):
        return lax.dot_general(
            left_rows, right_half, (((0,), (0,)), ((), ())), preferred_element_type=f32
        ).astype(bf16)

    def chip_scatter(whole, order):
        sizes = [grid_axes()[a][3] for a in "zxy"]
        rows = whole.shape[0] // (sizes[0] * sizes[1] * sizes[2])
        whole = whole.reshape(*sizes, rows, whole.shape[1])
        return Scatter(whole, order)

    def join_rows(flights):
        joined = Scatter(
            jnp.concatenate([f.whole for f in flights], axis=-2), flights[0].order, "z"
        )
        joined.parts = [f.whole.shape[-2] for f in flights]
        return joined

    def split_rows(flight):
        whole = run_out(flight)
        pieces, start = [], 0
        for rows in flight.parts:
            pieces.append(whole[start : start + rows])
            start += rows
        return pieces

    def shards_of(pieces):
        halves = [p.reshape(2, p.shape[0] // 2, p.shape[1]) for p in pieces]
        sent = jnp.concatenate(
            [lax.dynamic_index_in_dim(h, 1 - core, 0, False) for h in halves], axis=0
        )
        sent = swap_cores(sent)
        shards, start = [], 0
        first = core == 0
        for h in halves:
            kept = lax.dynamic_index_in_dim(h, core, 0, False)
            came = sent[start : start + h.shape[1]]
            start += h.shape[1]
            shards.append((jnp.where(first, kept, came), jnp.where(first, came, kept)))
        return shards

    down_grad = chip_grad(hidden, out_grad)
    down_shard = lax.psum_scatter(down_grad, everywhere, scatter_dimension=0, tiled=True)
    my_tile = pl.BlockSpec(tokens_tile, lambda j, core: (0, jnp.minimum(j, tiles // 2 - 1)))
    other_tile = pl.BlockSpec(tokens_tile, lambda j, core: (0, jnp.maximum(j - tiles // 2, 0)))
    tile_at = pl.BlockSpec(tokens_tile, lambda j, core: (0, turned(j, core)))
    half_array = array((token_count, ff_width // 2), bf16)
    gate_my, gate_other, up_my, up_other = feature_call(
        hidden_grad_kernel,
        core_number,
        tiles,
        [after(out_grad, down_grad), full_mlp_down, mlp_act, mlp_rise],
        [
            whole_spec(tokens_model),
            pl.BlockSpec((tile, model_width), lambda j, core: (turned(j, core), 0)),
            tile_at,
            tile_at,
        ],
        [half_array] * 4,
        [my_tile, other_tile, my_tile, other_tile],
    )
    gate_my, gate_other, up_my, up_other, hidden = lax.optimization_barrier(
        (gate_my, gate_other, up_my, up_other, hidden)
    )
    normed_mid_pair = both_rows(normed_mid)
    gate_grad_half = jnp.concatenate([gate_my, swap_cores(gate_other)], axis=0)
    up_grad_half = jnp.concatenate([up_my, swap_cores(up_other)], axis=0)
    (block_out,) = feature_call(
        down_kernel,
        core_number,
        tiles,
        [hidden, full_mlp_down, middle],
        [
            plain,
            pl.BlockSpec((tile, model_width), lambda j, core: (j, 0)),
            whole_spec(tokens_model),
        ],
        [array(tokens_model, f32)],
        [whole_spec(tokens_model)],
    )
    block_out, gate_grad_half, up_grad_half, normed_mid_pair = lax.optimization_barrier(
        (block_out, gate_grad_half, up_grad_half, normed_mid_pair)
    )
    mlp_gate_grad = chip_grad(normed_mid_pair, gate_grad_half)
    mlp_up_grad = chip_grad(normed_mid_pair, up_grad_half)
    gate_my, mlp_gate_grad, mlp_up_grad = lax.optimization_barrier(
        (gate_my, mlp_gate_grad, mlp_up_grad)
    )
    gate_flight = chip_scatter(mlp_gate_grad, "xzy")
    up_flight = chip_scatter(mlp_up_grad, "yxz")
    gate_my = launch(gate_my, gate_flight, up_flight)
    transposed = (((1,), (1,)), ((), ()))
    tokens_half = (token_count, model_width // 2)
    middle_grad, middle_low, middle_my, middle_other, gain_mid_grad = feature_call(
        middle_kernel,
        core_number,
        tiles,
        [
            gate_my,
            gate_other,
            up_my,
            up_other,
            full_mlp,
            full_mlp,
            middle,
            out_grad,
            gain_mid[None],
        ],
        [
            my_tile,
            other_tile,
            my_tile,
            other_tile,
            pl.BlockSpec((model_width, tile), lambda j, core: (0, turned(j, core))),
            pl.BlockSpec((model_width, tile), lambda j, core: (0, turned(j, core) + tiles)),
            whole_spec(tokens_model),
            whole_spec(tokens_model),
            whole_spec((1, model_width)),
        ],
        [
            array(tokens_model, f32),
            array(tokens_model, bf16),
            array(tokens_half, bf16),
            array(tokens_half, bf16),
            array((1, model_width), f32),
        ],
        [
            whole_spec(tokens_model),
            whole_spec(tokens_model),
            whole_spec(tokens_half),
            whole_spec(tokens_half),
            whole_spec((1, model_width)),
        ],
        [pltpu.VMEM(tokens_model, f32)],
    )

    def norm_back(grad, values, scale, gain):
        weighted = grad * gain
        inner = jnp.mean(weighted * values, axis=-1, keepdims=True)
        back = scale * weighted - values * (scale * scale * scale * inner)
        return back, jnp.sum(grad * values * scale, axis=0)

    middle_half = jnp.concatenate([middle_my, swap_cores(middle_other)], axis=0)
    mixed_pair = both_rows(mixed)
    mixed_grad = lax.dot_general(middle_low, full_branch, transposed, preferred_element_type=f32)
    gate_pre_low, tail_keep, local_grad = channel_call(
        reverse_kernel,
        row_count,
        [mixed_grad, states, gate_pre, keep],
        [wide_bf16, wide_f32, wide_f32],
        lru_width,
        block_width,
        kernel_flops,
    )
    normed_in_pair = both_rows(normed_in)
    first_keep = keep.reshape(row_count, row_tokens, lru_width)[:, 0]
    head_factor = first_keep * tail_keep.reshape(row_count, row_tokens, lru_width)[:, 0]
    head_grad = first_keep * local_grad.reshape(row_count, row_tokens, lru_width)[:, 0]
    grad_in = carry_before(head_factor, head_grad, True)
    grad_in, gate_pre_low, mixed_pair = tick(
        (grad_in, gate_pre_low, mixed_pair), gate_flight, up_flight
    )
    branch_grad = chip_grad(mixed_pair, middle_half)
    gate_in_grad = chip_grad(normed_in_pair, both_halves(gate_pre_low))
    grad_in, branch_grad, gate_in_grad = lax.optimization_barrier(
        (grad_in, branch_grad, gate_in_grad)
    )
    branch_flight = chip_scatter(branch_grad, "xyz")
    gate_in_flight = chip_scatter(gate_in_grad, "yxz")
    grad_in = launch(grad_in, branch_flight, gate_in_flight)
    square = jax.ShapeDtypeStruct((lru_width, block_width), f32)
    signal_part, head_part, rec_full, input_full, sums = channel_call(
        backward_kernel,
        row_count,
        [
            signal,
            before,
            masks,
            taps,
            rate,
            full_rec,
            full_input,
            conv_low,
            states,
            state_in,
            tail_keep,
            local_grad,
            grad_in,
        ],
        [
            wide_f32,
            jax.ShapeDtypeStruct((row_count * halo, lru_width), f32),
            square,
            square,
            jax.ShapeDtypeStruct((tap_count + 1, lru_width), f32),
        ],
        lru_width,
        block_width,
        3 * kernel_flops // 2,
    )
    signal_part = land(signal_part, gate_flight, up_flight)
    from_right = passed_along(
        head_part.reshape(row_count, halo, lru_width)[:, halo - halo_rows :].astype(bf16),
        "seq",
        -1,
    ).astype(f32)
    signal_low = (
        (
            signal_part.reshape(row_count, row_tokens, lru_width)
            + jnp.pad(from_right, ((0, 0), (row_tokens - halo_rows, 0), (0, 0)))
        )
        .astype(bf16)
        .reshape(token_count, lru_width)
    )
    signal_low = launch(signal_low, gate_flight, up_flight)
    signal_low, gate_pre_low, signal_half = lax.optimization_barrier(
        (signal_low, gate_pre_low, my_half(signal_low))
    )
    gate_part = lax.dot_general(
        gate_pre_low, full_gate_in, transposed, preferred_element_type=f32
    )
    gate_part, sent_half = lax.optimization_barrier(
        (gate_part, swap_cores(other_half(signal_low)))
    )
    signal_grad = chip_grad(
        normed_in_pair, jnp.concatenate([signal_half, sent_half], axis=0)
    )
    pair_grads = jnp.where(core == 0, rec_full, input_full) + swap_cores(
        jnp.where(core == 0, input_full, rec_full).astype(bf16)
    ).astype(f32)
    sizes = [grid_axes()[a][3] for a in "zxyc"]
    chip_count = sizes[0] * sizes[1] * sizes[2]
    quarter = lru_width // 4
    signal_first = chip_scatter(signal_grad[:, :quarter], "xyz")
    pair_rows = pair_grads.astype(bf16).reshape(chip_count, -1, quarter)
    pair_count = pair_rows.shape[1]
    signal_second = chip_scatter(
        jnp.concatenate(
            [signal_grad[:, quarter:].reshape(chip_count, -1, quarter), pair_rows], axis=1
        ).reshape(-1, quarter),
        "yxz",
    )
    signal_low = launch(signal_low, signal_first, signal_second)
    normed_in_grad = gate_part + lax.dot_general(
        signal_low, full_signal, transposed, preferred_element_type=f32
    )
    normed_in_grad = tick(
        after(normed_in_grad, down_shard),
        signal_first,
        signal_second,
        branch_flight,
        gate_in_flight,
    )
    normed_in_grad = land(normed_in_grad, gate_flight, up_flight)
    in_back, gain_in_grad = norm_back(normed_in_grad, inputs, scale_in, gain_in)
    in_back, gain_in_grad = land((in_back, gain_in_grad), signal_first, signal_second)
    signal_last = join_rows([signal_first, signal_second])
    in_back, gain_in_grad = launch((in_back, gain_in_grad), signal_last)
    in_back = land(in_back, branch_flight, gate_in_flight)
    branch_rows = branch_flight.whole.shape[-2]
    branch_flight.whole = branch_flight.whole.reshape(sizes[0], -1, lru_half)
    middle_two = join_rows([branch_flight, gate_in_flight])
    in_back = launch(in_back, middle_two)
    tokens_grad = (middle_grad + in_back).reshape(tokens.shape)

    decay_grad = sums[0] * rate_scale * jax.nn.sigmoid(-decay_full)
    small_grads = [gain_in_grad, gain_mid_grad[0], decay_grad, *(sums[1 + k] for k in range(tap_count))]
    every_small = jnp.concatenate(small_grads)
    for which in "cxyz":
        every_small = every_small + sum(
            hop(every_small, which, d) for d in range(1, grid_axes()[which][3])
        )
    device = lax.axis_index("dp") * lax.axis_size("seq") + lax.axis_index("seq")
    small_shards, start = [], 0
    for grad in small_grads:
        width = grad.shape[0] // device_count
        small_shards.append(
            lax.dynamic_slice_in_dim(every_small, start + device * width, width, 0)
        )
        start += grad.shape[0]
    mlp_gate_shard, mlp_up_shard = [
        jnp.concatenate(pair, axis=1)
        for pair in shards_of([gate_flight.whole, up_flight.whole])
    ]
    branch_pair, gate_in_pair = shards_of(split_rows(middle_two))
    branch_shard = jnp.concatenate(
        [a.reshape(-1, model_width // 2) for a in branch_pair], axis=1
    )
    gate_in_shard = jnp.concatenate(gate_in_pair, axis=1)
    signal_last.parts = [
        signal_last.parts[0],
        signal_last.parts[1] - pair_count,
        pair_count,
    ]
    signal_one, signal_two, pair_halves = shards_of(split_rows(signal_last))
    signal_shard = jnp.concatenate(
        [signal_one[0], signal_two[0], signal_one[1], signal_two[1]], axis=1
    )
    return (
        block_out.reshape(tokens.shape),
        tokens_grad,
        small_shards[0],
        gate_in_shard,
        signal_shard,
        jnp.stack(small_shards[3:]),
        pair_halves[0].reshape(lru_piece, block_width),
        pair_halves[1].reshape(lru_piece, block_width),
        small_shards[2],
        branch_shard,
        small_shards[1],
        mlp_gate_shard,
        mlp_up_shard,
        down_shard.astype(f32),
    )


def solution(mesh):
    rows = P(("dp", "seq"))
    matrix = P(("dp", "seq"), None)
    columns = P(None, ("dp", "seq"))
    tokens = P("dp", "seq", None)
    return jax.shard_map(
        body,
        mesh=mesh,
        in_specs=(
            tokens,
            P("dp", "seq"),
            rows,
            matrix,
            matrix,
            columns,
            matrix,
            matrix,
            rows,
            matrix,
            rows,
            matrix,
            matrix,
            matrix,
            tokens,
        ),
        out_specs=(
            tokens,
            tokens,
            rows,
            matrix,
            matrix,
            columns,
            matrix,
            matrix,
            rows,
            matrix,
            rows,
            matrix,
            matrix,
            matrix,
        ),
        check_vma=False,
    )
```

```python
import functools

import jax
import jax.numpy as jnp
from jax import lax
from jax.experimental import pallas as pl
from jax.experimental.pallas import tpu as pltpu
from jax.sharding import PartitionSpec as P

epsilon = 1e-06
rate_scale = 8.0
f32 = jnp.float32
bf16 = jnp.bfloat16
gelu_rate = 0.7978845608028654
gelu_cube = 0.044715
halo = 8
mib = 1024 * 1024


def grid_axes():
    dp, seq = lax.axis_size("dp"), lax.axis_size("seq")
    return {
        "z": ("dp", dp, 2, dp // 2),
        "x": ("dp", dp, 1, 2),
        "y": ("seq", seq, 2, seq // 2),
        "c": ("seq", seq, 1, 2),
    }


def place_on(which):
    name, _, stride, count = grid_axes()[which]
    return lax.rem(lax.div(lax.axis_index(name), stride), count)


def ring_step(block, which):
    name, total, stride, count = grid_axes()[which]
    route = []
    for i in range(total):
        k = (i // stride) % count
        route.append((i, i + ((k + 1) % count - k) * stride))
    return lax.ppermute(block, name, route)


def swap_cores(block):
    return ring_step(block, "c")


def passed_along(block, axis, distance):
    devices = range(lax.axis_size(axis))
    route = [(i - distance, i) for i in devices if i - distance in devices]
    return lax.ppermute(block, axis, route)


def after(value, *others):
    return lax.optimization_barrier((value, *others))[0]


def hop(block, which, distance):
    name, total, stride, count = grid_axes()[which]
    route = []
    for i in range(total):
        k = (i // stride) % count
        route.append((i, i + ((k + distance) % count - k) * stride))
    return lax.ppermute(block, name, route)


class Flight:
    def done(self):
        return not self.order


class Gather(Flight):
    def __init__(self, piece, order):
        self.piece = piece
        self.order = list(order)
        self.have = []

    def sends(self, which):
        return [self.piece] * (grid_axes()[which][3] - 1)

    def finish(self):
        which = self.order.pop(0)
        count = grid_axes()[which][3]
        me = place_on(which)
        spot = sum(1 for other in self.have if "zxyc".index(other) < "zxyc".index(which))
        piece = self.piece
        parts = [piece] + self.moved
        if count == 2:
            first = me == 0
            a, b = parts
            piece = jnp.stack([jnp.where(first, a, b), jnp.where(first, b, a)], axis=spot)
        else:
            stacked = jnp.zeros(piece.shape[:spot] + (count,) + piece.shape[spot:], piece.dtype)
            for t, part in enumerate(parts):
                stacked = lax.dynamic_update_index_in_dim(
                    stacked, part, lax.rem(me - t + count, count), spot
                )
            piece = stacked
        self.have.append(which)
        self.piece = piece


class Scatter(Flight):
    def __init__(self, whole, order, left="zxy"):
        self.whole = whole
        self.wide = whole.dtype
        self.order = list(order)
        self.left = list(left)

    def own(self, ahead):
        which = self.order[0]
        count = grid_axes()[which][3]
        return lax.dynamic_index_in_dim(
            self.whole,
            lax.rem(place_on(which) + ahead, count),
            self.left.index(which),
            False,
        )

    def sends(self, which):
        return [self.own(d) for d in range(1, grid_axes()[which][3])]

    def finish(self):
        total = self.own(0).astype(f32)
        for moved in self.moved:
            total = total + moved.astype(f32)
        self.left.remove(self.order.pop(0))
        self.whole = total.astype(self.wide) if self.order else total


def launch(value, *flights):
    blocks = [f.sends(f.order[0]) for f in flights]
    value, blocks = lax.optimization_barrier((value, blocks))
    for f, sent in zip(flights, blocks):
        which = f.order[0]
        f.moved = [hop(block, which, d + 1) for d, block in enumerate(sent)]
    return value


def land(value, *flights):
    value, landed = lax.optimization_barrier((value, [f.moved for f in flights]))
    for f, moved in zip(flights, landed):
        f.moved = moved
        f.finish()
    return value


def tick(value, *flights):
    value = land(value, *flights)
    return launch(value, *[f for f in flights if not f.done()])


def run_out(flight):
    if not flight.done():
        flight.finish()
    while not flight.done():
        launch(None, flight)
        flight.finish()
    return flight.whole


def gelu_parts(v):
    th = jnp.tanh(gelu_rate * (v + gelu_cube * v * v * v))
    value = 0.5 * v * (1.0 + th)
    slope = 0.5 * (1.0 + th) + 0.5 * v * (1.0 - th * th) * gelu_rate * (
        1.0 + 3.0 * gelu_cube * v * v
    )
    return value, slope


def scan_rows(a, b, reverse):
    count, width = a.shape
    a, b = a.reshape(-1, 8, width), b.reshape(-1, 8, width)
    row = lax.broadcasted_iota(jnp.int32, a.shape, 1)
    for s in (1, 2, 4):
        shift = 8 - s if reverse else s
        valid = row < 8 - s if reverse else row >= s
        a_far = pltpu.roll(a, shift, 1)
        b_far = pltpu.roll(b, shift, 1)
        b = jnp.where(valid, a * b_far + b, b)
        a = jnp.where(valid, a * a_far, a)
    edge = 0 if reverse else 7
    a_all, b_all = a[:, edge], b[:, edge]
    groups = count // 8
    one, zero = jnp.ones_like(a_all[:1]), jnp.zeros_like(a_all[:1])
    s = 1
    while s < groups:
        if reverse:
            a_far = jnp.concatenate([a_all[s:], jnp.broadcast_to(one, (s, width))], axis=0)
            b_far = jnp.concatenate([b_all[s:], jnp.broadcast_to(zero, (s, width))], axis=0)
        else:
            a_far = jnp.concatenate([jnp.broadcast_to(one, (s, width)), a_all[:-s]], axis=0)
            b_far = jnp.concatenate([jnp.broadcast_to(zero, (s, width)), b_all[:-s]], axis=0)
        b_all = a_all * b_far + b_all
        a_all = a_all * a_far
        s *= 2
    if reverse:
        a_in = jnp.concatenate([a_all[1:], one], axis=0)
        b_in = jnp.concatenate([b_all[1:], zero], axis=0)
    else:
        a_in = jnp.concatenate([one, a_all[:-1]], axis=0)
        b_in = jnp.concatenate([zero, b_all[:-1]], axis=0)
    b = a * b_in[:, None] + b
    a = a * a_in[:, None]
    return a.reshape(count, width), b.reshape(count, width)


def sigmoid(x):
    return 0.5 + 0.5 * jnp.tanh(0.5 * x)


def minus_expm1(x):
    t = 1.0 / 5040.0
    for k in (720.0, 120.0, 24.0, 6.0, 2.0):
        t = t * x + 1.0 / k
    return -x * (t * x + 1.0)


def gate_values(conv_low, rec_w, inp_w, rate, reset):
    r = sigmoid(jnp.dot(conv_low, rec_w, preferred_element_type=f32))
    g = sigmoid(jnp.dot(conv_low, inp_w, preferred_element_type=f32))
    log_keep = rate * (0.1 + 0.9 * r)
    keep = jnp.where(reset, 0.0, jnp.exp(log_keep))
    lost = minus_expm1(2.0 * log_keep)
    inverse = lax.rsqrt(lost)
    scale = jnp.where(reset, 1.0, lost * inverse)
    return r, g, keep, lost, inverse, scale


def forward_kernel(
    row_count,
    sig_ref,
    tail_ref,
    mask_ref,
    taps_ref,
    rate_ref,
    rec_ref,
    inp_ref,
    conv_ref,
    keep_ref,
    cum_ref,
    local_ref,
):
    row_tokens = sig_ref.shape[0] // row_count
    for b in range(row_count):
        rows = pl.ds(b * row_tokens, row_tokens)
        sig = sig_ref[rows, :].astype(f32)
        ext = jnp.concatenate([tail_ref[pl.ds(b * halo, halo), :], sig], axis=0)
        conv = taps_ref[0:1, :] * sig
        for k in range(1, taps_ref.shape[0]):
            conv += taps_ref[k : k + 1, :] * pltpu.roll(ext, k, 0)[halo:] * mask_ref[k - 1, rows, :]
        conv_low = conv.astype(bf16)
        conv_ref[rows, :] = conv_low
        reset = mask_ref[0, rows, :] == 0.0
        _, g, keep, _, _, scale = gate_values(
            conv_low, rec_ref[...], inp_ref[...], rate_ref[...], reset
        )
        keep_ref[rows, :] = keep
        cum, local = scan_rows(keep, scale * conv_low.astype(f32) * g, False)
        cum_ref[rows, :] = cum
        local_ref[rows, :] = local


def reverse_kernel(
    row_count, mixed_grad_ref, states_ref, gate_ref, keep_ref, gate_low_ref, tail_ref, local_ref
):
    row_tokens = keep_ref.shape[0] // row_count
    for b in range(row_count):
        rows = pl.ds(b * row_tokens, row_tokens)
        value, slope = gelu_parts(gate_ref[rows, :])
        grad = mixed_grad_ref[rows, :]
        gate_low_ref[rows, :] = (grad * states_ref[rows, :] * slope).astype(bf16)
        keep = keep_ref[rows, :]
        row = lax.broadcasted_iota(jnp.int32, keep.shape, 0)
        next_keep = jnp.where(row == row_tokens - 1, 1.0, pltpu.roll(keep, row_tokens - 1, 0))
        tail, local = scan_rows(next_keep, grad * value, True)
        tail_ref[rows, :] = tail
        local_ref[rows, :] = local


def backward_kernel(
    row_count,
    sig_ref,
    before_ref,
    mask_ref,
    taps_ref,
    rate_ref,
    rec_ref,
    inp_ref,
    conv_ref,
    states_ref,
    state_in_ref,
    tail_ref,
    local_ref,
    grad_in_ref,
    signal_ref,
    head_ref,
    rec_grad_ref,
    inp_grad_ref,
    sums_ref,
):
    row_tokens = sig_ref.shape[0] // row_count
    tap_count = taps_ref.shape[0]
    rate = rate_ref[...]
    sums = [0.0] * (tap_count + 1)
    rec_total = 0.0
    inp_total = 0.0
    for b in range(row_count):
        rows = pl.ds(b * row_tokens, row_tokens)
        conv_low = conv_ref[rows, :]
        conv = conv_low.astype(f32)
        reset = mask_ref[0, rows, :] == 0.0
        r, g, keep, lost, inverse, scale = gate_values(
            conv_low, rec_ref[...], inp_ref[...], rate, reset
        )
        state_grad = local_ref[rows, :] + tail_ref[rows, :] * grad_in_ref[b : b + 1, :]
        states = states_ref[rows, :]
        row = lax.broadcasted_iota(jnp.int32, states.shape, 0)
        before = jnp.where(row == 0, state_in_ref[b : b + 1, :], pltpu.roll(states, 1, 0))
        direct = state_grad * g
        dlog = state_grad * before * keep - jnp.where(
            reset, 0.0, direct * conv * (1.0 - lost) * inverse
        )
        rec_low = (dlog * rate * 0.9 * r * (1.0 - r)).astype(bf16)
        input_low = (direct * scale * conv * (1.0 - g)).astype(bf16)
        sums[0] += jnp.sum(dlog * (0.1 + 0.9 * r), axis=0, keepdims=True)
        first = (((0,), (0,)), ((), ()))
        second = (((1,), (1,)), ((), ()))
        rec_total += lax.dot_general(conv_low, rec_low, first, preferred_element_type=f32)
        inp_total += lax.dot_general(conv_low, input_low, first, preferred_element_type=f32)
        conv_grad = (
            direct * scale
            + lax.dot_general(rec_low, rec_ref[...], second, preferred_element_type=f32)
            + lax.dot_general(input_low, inp_ref[...], second, preferred_element_type=f32)
        )
        sig = sig_ref[rows, :].astype(f32)
        ext = jnp.concatenate([before_ref[pl.ds(b * halo, halo), :], sig], axis=0)
        blank = jnp.zeros((halo, sig.shape[1]), f32)
        back = jnp.concatenate([blank, conv_grad * taps_ref[0:1, :]], axis=0)
        sums[1] += jnp.sum(conv_grad * sig, axis=0, keepdims=True)
        for k in range(1, tap_count):
            part = conv_grad * mask_ref[k - 1, rows, :]
            sums[1 + k] += jnp.sum(part * pltpu.roll(ext, k, 0)[halo:], axis=0, keepdims=True)
            moved = jnp.concatenate([blank, part * taps_ref[k : k + 1, :]], axis=0)
            back += pltpu.roll(moved, row_tokens + halo - k, 0)
        head_ref[pl.ds(b * halo, halo), :] = back[:halo]
        signal_ref[rows, :] = back[halo:]
    rec_grad_ref[...] = rec_total
    inp_grad_ref[...] = inp_total
    for k in range(tap_count + 1):
        sums_ref[k : k + 1, :] = sums[k]


def channel_call(kernel, row_count, ins, outs, width, block, flops):
    def spec(shape):
        if len(shape) == 3:
            return pl.BlockSpec((shape[0], shape[1], block), lambda h: (0, 0, 0))
        if shape == (width, block):
            return pl.BlockSpec((block, block), lambda h: (h, 0))
        return pl.BlockSpec((shape[0], block), lambda h: (0, h))

    return pl.pallas_call(
        functools.partial(kernel, row_count),
        grid=(width // block,),
        in_specs=[spec(a.shape) for a in ins],
        out_specs=[spec(o.shape) for o in outs],
        out_shape=outs,
        compiler_params=pltpu.CompilerParams(vmem_limit_bytes=14 * mib),
        cost_estimate=pl.CostEstimate(flops=flops, bytes_accessed=1, transcendentals=0),
    )(*ins)


def feature_call(kernel, room, core, grid, ins, in_specs, outs, out_specs, scratch=()):
    return pl.pallas_call(
        kernel,
        grid_spec=pltpu.PrefetchScalarGridSpec(
            num_scalar_prefetch=1,
            grid=(grid,),
            in_specs=in_specs,
            out_specs=out_specs,
            scratch_shapes=list(scratch),
        ),
        out_shape=outs,
        compiler_params=pltpu.CompilerParams(vmem_limit_bytes=48 * mib),
        cost_estimate=pl.CostEstimate(flops=1, bytes_accessed=1, transcendentals=0),
    )(core, *ins)


def whole_spec(shape):
    return pl.BlockSpec(shape, lambda j, core: (0,) * len(shape))


def mlp_kernel(core_ref, normed_ref, gate_w_ref, up_w_ref, act_ref, rise_ref, hidden_ref):
    normed = normed_ref[...]
    gate = jnp.dot(normed, gate_w_ref[...], preferred_element_type=f32)
    up = jnp.dot(normed, up_w_ref[...], preferred_element_type=f32)
    value, slope = gelu_parts(gate)
    act_ref[...] = value.astype(bf16)
    rise_ref[...] = (up * slope).astype(bf16)
    hidden_ref[...] = (value * up).astype(bf16)


def down_kernel(core_ref, hidden_ref, down_ref, middle_ref, out_ref):
    @pl.when(pl.program_id(0) == 0)
    def _():
        out_ref[...] = middle_ref[...]

    out_ref[...] += jnp.dot(hidden_ref[...], down_ref[...], preferred_element_type=f32)


def hidden_grad_kernel(
    core_ref, grad_ref, down_ref, act_ref, rise_ref, gate_my, gate_other, up_my, up_other
):
    grad = lax.dot_general(
        grad_ref[...], down_ref[...], (((1,), (1,)), ((), ())), preferred_element_type=f32
    )
    gate_low = (grad * rise_ref[...]).astype(bf16)
    up_low = (grad * act_ref[...]).astype(bf16)
    mine = pl.program_id(0) < pl.num_programs(0) // 2

    @pl.when(mine)
    def _():
        gate_my[...] = gate_low
        up_my[...] = up_low

    @pl.when(jnp.logical_not(mine))
    def _():
        gate_other[...] = gate_low
        up_other[...] = up_low


def middle_kernel(
    core_ref,
    gate_my,
    gate_other,
    up_my,
    up_other,
    gate_w_ref,
    up_w_ref,
    middle_ref,
    grad_ref,
    gain_ref,
    middle_grad_ref,
    low_ref,
    low_my,
    low_other,
    gain_grad_ref,
    total,
):
    j = pl.program_id(0)
    transposed = (((1,), (1,)), ((), ()))

    @pl.when(j == 0)
    def _():
        total[...] = jnp.zeros_like(total)

    def add(gate_ref, up_ref):
        total[...] += lax.dot_general(
            gate_ref[...], gate_w_ref[...], transposed, preferred_element_type=f32
        ) + lax.dot_general(up_ref[...], up_w_ref[...], transposed, preferred_element_type=f32)

    mine = j < pl.num_programs(0) // 2

    @pl.when(mine)
    def _():
        add(gate_my, up_my)

    @pl.when(jnp.logical_not(mine))
    def _():
        add(gate_other, up_other)

    @pl.when(j == pl.num_programs(0) - 1)
    def _():
        middle = middle_ref[...]
        scale = lax.rsqrt(jnp.mean(middle * middle, axis=-1, keepdims=True) + epsilon)
        grad = total[...]
        weighted = grad * gain_ref[...]
        inner = jnp.mean(weighted * middle, axis=-1, keepdims=True)
        back = scale * weighted - middle * (scale * scale * scale * inner)
        middle_grad = grad_ref[...].astype(f32) + back
        middle_grad_ref[...] = middle_grad
        low = middle_grad.astype(bf16)
        low_ref[...] = low
        half = low.shape[1] // 2
        first = core_ref[0] == 0

        @pl.when(first)
        def _():
            low_my[...] = low[:, :half]
            low_other[...] = low[:, half:]

        @pl.when(jnp.logical_not(first))
        def _():
            low_my[...] = low[:, half:]
            low_other[...] = low[:, :half]

        gain_grad_ref[...] = jnp.sum(grad * middle * scale, axis=0, keepdims=True)


def carry_before(factor, value, reverse):
    count = lax.axis_size("seq")
    place = lax.axis_index("seq")
    both = lax.all_gather(jnp.stack([factor, value]), "seq")
    state = jnp.zeros_like(value)
    turns = range(count - 1, 0, -1) if reverse else range(count - 1)
    for source in turns:
        passed = place < source if reverse else source < place
        state = jnp.where(passed, both[source, 0] * state + both[source, 1], state)
    return state


def body(
    tokens,
    segments,
    norm_in_gain,
    gate_in_weight,
    signal_in_weight,
    conv_weight,
    rec_gate_weight,
    input_gate_weight,
    decay_param,
    branch_out_weight,
    norm_mid_gain,
    mlp_gate_weight,
    mlp_up_weight,
    mlp_down_weight,
    cotangent,
):
    row_count, row_tokens, model_width = tokens.shape
    lru_width = signal_in_weight.shape[1]
    block_width = rec_gate_weight.shape[1]
    ff_width = mlp_gate_weight.shape[1]
    tap_count = conv_weight.shape[0]
    halo_rows = tap_count - 1
    token_count = row_count * row_tokens
    device_count = lax.axis_size("dp") * lax.axis_size("seq")
    core = place_on("c")
    model_piece = norm_in_gain.shape[0]
    lru_piece = decay_param.shape[0]

    small = jnp.concatenate(
        [
            rec_gate_weight.reshape(-1),
            input_gate_weight.reshape(-1),
            norm_in_gain,
            norm_mid_gain,
            decay_param,
            conv_weight.reshape(-1),
        ]
    )
    pack_width = -(-small.shape[0] // (model_piece * 128)) * 128
    pack = jnp.pad(small, (0, model_piece * pack_width - small.shape[0]))
    pack = pack.reshape(model_piece, pack_width)
    everywhere = ("dp", "seq")
    lru_half = lru_width // 2
    mlp_pair = jnp.concatenate([mlp_gate_weight, mlp_up_weight], axis=1)
    full_mlp = lax.all_gather(mlp_pair, everywhere, axis=0, tiled=True)
    full_mlp_down = lax.all_gather(mlp_down_weight, everywhere, axis=0, tiled=True)
    s1 = Gather(signal_in_weight[:, :lru_half], "zyxc")
    s2 = Gather(jnp.concatenate([signal_in_weight[:, lru_half:], pack], axis=1), "zxyc")
    launch(None, s1, s2)
    tick(None, s1, s2)
    gi = Gather(after(gate_in_weight, s1.piece), "zxyc")
    br = Gather(after(branch_out_weight, s1.piece), "zyxc")
    launch(None, gi, br)
    tick(None, s1, s2)
    tick(None, s1, s2, gi, br)
    land(None, s1, s2)
    smalls = s2.piece.reshape(model_width, -1)
    full_signal = jnp.concatenate(
        [s1.piece.reshape(model_width, -1), smalls[:, :lru_half]], axis=1
    )
    smalls = smalls[:, lru_half:].reshape(device_count, model_piece * pack_width)
    gate_size = lru_piece * block_width
    full_rec = smalls[:, :gate_size].reshape(lru_width, block_width)
    full_input = smalls[:, gate_size : 2 * gate_size].reshape(lru_width, block_width)
    smalls = smalls[:, 2 * gate_size :].astype(f32)
    gain_in = smalls[:, :model_piece].reshape(model_width)
    gain_mid = smalls[:, model_piece : 2 * model_piece].reshape(model_width)
    start = 2 * model_piece
    decay_full = smalls[:, start : start + lru_piece].reshape(lru_width)
    start += lru_piece
    taps = (
        smalls[:, start : start + tap_count * lru_piece]
        .reshape(device_count, tap_count, lru_piece)
        .transpose(1, 0, 2)
        .reshape(tap_count, lru_width)
    )
    rate = (-rate_scale * jax.nn.softplus(-decay_full))[None, :]

    def other_half(a):
        width = a.shape[1] // 2
        return lax.dynamic_slice_in_dim(a, (1 - core) * width, width, 1)

    def my_half(a):
        width = a.shape[1] // 2
        return lax.dynamic_slice_in_dim(a, core * width, width, 1)

    def both_rows(a):
        return jnp.concatenate([a, swap_cores(a)], axis=0)

    def both_halves(a):
        return jnp.concatenate([my_half(a), swap_cores(other_half(a))], axis=0)

    out_grad = cotangent.reshape(token_count, model_width)

    inputs = tokens.astype(f32).reshape(token_count, model_width)
    tail_tokens = passed_along(tokens[:, row_tokens - halo_rows :], "seq", 1)

    def norm_scale(values):
        return lax.rsqrt(jnp.mean(values * values, axis=-1, keepdims=True) + epsilon)

    scale_in = norm_scale(inputs)
    normed_in = (inputs * scale_in * gain_in).astype(bf16)
    tail_rows = jnp.pad(tail_tokens.astype(f32), ((0, 0), (halo - halo_rows, 0), (0, 0)))
    tail_rows = tail_rows.reshape(row_count * halo, model_width)
    tail_normed = (tail_rows * norm_scale(tail_rows) * gain_in).astype(bf16)
    before = (
        jnp.dot(tail_normed, full_signal, preferred_element_type=f32).astype(bf16).astype(f32)
    )
    signal = jnp.dot(normed_in, full_signal, preferred_element_type=f32).astype(bf16)
    tail_ids = passed_along(segments[:, row_tokens - halo_rows :], "seq", 1)
    tail_ids = jnp.where(lax.axis_index("seq") == 0, jnp.int32(-1), tail_ids)
    ids_ext = jnp.concatenate([tail_ids, segments], axis=1)
    masks = jnp.stack(
        [
            (ids_ext[:, halo_rows - k : halo_rows - k + row_tokens] == segments).astype(f32)
            for k in range(1, tap_count)
        ]
    )
    masks = jnp.broadcast_to(
        masks.reshape(halo_rows, token_count, 1), (halo_rows, token_count, block_width)
    )

    wide_f32 = jax.ShapeDtypeStruct((token_count, lru_width), f32)
    wide_bf16 = jax.ShapeDtypeStruct((token_count, lru_width), bf16)
    kernel_flops = 1
    conv_low, keep, cum_keep, local_state = channel_call(
        forward_kernel,
        row_count,
        [signal, before, masks, taps, rate, full_rec, full_input],
        [wide_bf16, wide_f32, wide_f32, wide_f32],
        lru_width,
        block_width,
        kernel_flops,
    )
    cum3 = cum_keep.reshape(row_count, row_tokens, lru_width)
    local3 = local_state.reshape(row_count, row_tokens, lru_width)
    state_in = carry_before(cum3[:, -1], local3[:, -1], False)
    state_in = tick(state_in, gi, br)
    state_in = land(tick(state_in, gi, br), gi, br)
    full_gate_in = gi.piece.reshape(model_width, lru_width)
    gate_pre = jnp.dot(normed_in, full_gate_in, preferred_element_type=f32)
    states = (local3 + cum3 * state_in[:, None, :]).reshape(token_count, lru_width)
    mixed = (gelu_parts(gate_pre)[0] * states).astype(bf16)
    full_branch = br.piece.reshape(lru_width, model_width)
    middle = inputs + jnp.dot(mixed, full_branch, preferred_element_type=f32)
    scale_mid = norm_scale(middle)
    normed_mid = (middle * scale_mid * gain_mid).astype(bf16)
    tile = 768
    tiles = ff_width // tile
    tokens_model = (token_count, model_width)
    tokens_tile = (token_count, tile)
    core_number = core.astype(jnp.int32).reshape(1)

    def turned(j, core):
        return lax.rem(j + core[0] * (tiles // 2), tiles)

    def array(shape, kind):
        return jax.ShapeDtypeStruct(shape, kind)

    plain = pl.BlockSpec(tokens_tile, lambda j, core: (0, j))
    mlp_act, mlp_rise, hidden = feature_call(
        mlp_kernel,
        22,
        core_number,
        tiles,
        [normed_mid, full_mlp, full_mlp],
        [
            whole_spec(tokens_model),
            pl.BlockSpec((model_width, tile), lambda j, core: (0, j)),
            pl.BlockSpec((model_width, tile), lambda j, core: (0, j + tiles)),
        ],
        [
            array((token_count, ff_width), bf16),
            array((token_count, ff_width), bf16),
            array((token_count, ff_width), bf16),
        ],
        [plain, plain, plain],
    )


    def chip_grad(left_rows, right_half):
        return lax.dot_general(
            left_rows, right_half, (((0,), (0,)), ((), ())), preferred_element_type=f32
        ).astype(bf16)

    def chip_scatter(whole, order):
        sizes = [grid_axes()[a][3] for a in "zxy"]
        rows = whole.shape[0] // (sizes[0] * sizes[1] * sizes[2])
        whole = whole.reshape(*sizes, rows, whole.shape[1])
        return Scatter(whole, order)

    def join_rows(flights):
        joined = Scatter(
            jnp.concatenate([f.whole for f in flights], axis=-2), flights[0].order, "z"
        )
        joined.parts = [f.whole.shape[-2] for f in flights]
        return joined

    def split_rows(flight):
        whole = run_out(flight)
        pieces, start = [], 0
        for rows in flight.parts:
            pieces.append(whole[start : start + rows])
            start += rows
        return pieces

    def shards_of(pieces):
        halves = [p.reshape(2, p.shape[0] // 2, p.shape[1]) for p in pieces]
        sent = jnp.concatenate(
            [lax.dynamic_index_in_dim(h, 1 - core, 0, False) for h in halves], axis=0
        )
        sent = swap_cores(sent)
        shards, start = [], 0
        first = core == 0
        for h in halves:
            kept = lax.dynamic_index_in_dim(h, core, 0, False)
            came = sent[start : start + h.shape[1]]
            start += h.shape[1]
            shards.append((jnp.where(first, kept, came), jnp.where(first, came, kept)))
        return shards

    down_grad = chip_grad(hidden, out_grad)
    down_shard = lax.psum_scatter(down_grad, everywhere, scatter_dimension=0, tiled=True)
    my_tile = pl.BlockSpec(tokens_tile, lambda j, core: (0, jnp.minimum(j, tiles // 2 - 1)))
    other_tile = pl.BlockSpec(tokens_tile, lambda j, core: (0, jnp.maximum(j - tiles // 2, 0)))
    tile_at = pl.BlockSpec(tokens_tile, lambda j, core: (0, turned(j, core)))
    half_array = array((token_count, ff_width // 2), bf16)
    gate_my, gate_other, up_my, up_other = feature_call(
        hidden_grad_kernel,
        18,
        core_number,
        tiles,
        [after(out_grad, down_grad), full_mlp_down, mlp_act, mlp_rise],
        [
            whole_spec(tokens_model),
            pl.BlockSpec((tile, model_width), lambda j, core: (turned(j, core), 0)),
            tile_at,
            tile_at,
        ],
        [half_array] * 4,
        [my_tile, other_tile, my_tile, other_tile],
    )
    gate_my, gate_other, up_my, up_other, hidden = lax.optimization_barrier(
        (gate_my, gate_other, up_my, up_other, hidden)
    )
    normed_mid_pair = both_rows(normed_mid)
    gate_grad_half = jnp.concatenate([gate_my, swap_cores(gate_other)], axis=0)
    up_grad_half = jnp.concatenate([up_my, swap_cores(up_other)], axis=0)
    (block_out,) = feature_call(
        down_kernel,
        16,
        core_number,
        tiles,
        [hidden, full_mlp_down, middle],
        [
            plain,
            pl.BlockSpec((tile, model_width), lambda j, core: (j, 0)),
            whole_spec(tokens_model),
        ],
        [array(tokens_model, f32)],
        [whole_spec(tokens_model)],
    )
    block_out, gate_grad_half, up_grad_half, normed_mid_pair = lax.optimization_barrier(
        (block_out, gate_grad_half, up_grad_half, normed_mid_pair)
    )
    mlp_gate_grad = chip_grad(normed_mid_pair, gate_grad_half)
    mlp_up_grad = chip_grad(normed_mid_pair, up_grad_half)
    gate_my, mlp_gate_grad, mlp_up_grad = lax.optimization_barrier(
        (gate_my, mlp_gate_grad, mlp_up_grad)
    )
    gate_flight = chip_scatter(mlp_gate_grad, "xzy")
    up_flight = chip_scatter(mlp_up_grad, "yxz")
    gate_my = launch(gate_my, gate_flight, up_flight)
    transposed = (((1,), (1,)), ((), ()))
    tokens_half = (token_count, model_width // 2)
    middle_grad, middle_low, middle_my, middle_other, gain_mid_grad = feature_call(
        middle_kernel,
        32,
        core_number,
        tiles,
        [
            gate_my,
            gate_other,
            up_my,
            up_other,
            full_mlp,
            full_mlp,
            middle,
            out_grad,
            gain_mid[None],
        ],
        [
            my_tile,
            other_tile,
            my_tile,
            other_tile,
            pl.BlockSpec((model_width, tile), lambda j, core: (0, turned(j, core))),
            pl.BlockSpec((model_width, tile), lambda j, core: (0, turned(j, core) + tiles)),
            whole_spec(tokens_model),
            whole_spec(tokens_model),
            whole_spec((1, model_width)),
        ],
        [
            array(tokens_model, f32),
            array(tokens_model, bf16),
            array(tokens_half, bf16),
            array(tokens_half, bf16),
            array((1, model_width), f32),
        ],
        [
            whole_spec(tokens_model),
            whole_spec(tokens_model),
            whole_spec(tokens_half),
            whole_spec(tokens_half),
            whole_spec((1, model_width)),
        ],
        [pltpu.VMEM(tokens_model, f32)],
    )

    def norm_back(grad, values, scale, gain):
        weighted = grad * gain
        inner = jnp.mean(weighted * values, axis=-1, keepdims=True)
        back = scale * weighted - values * (scale * scale * scale * inner)
        return back, jnp.sum(grad * values * scale, axis=0)

    middle_half = jnp.concatenate([middle_my, swap_cores(middle_other)], axis=0)
    mixed_pair = both_rows(mixed)
    mixed_grad = lax.dot_general(middle_low, full_branch, transposed, preferred_element_type=f32)
    gate_pre_low, tail_keep, local_grad = channel_call(
        reverse_kernel,
        row_count,
        [mixed_grad, states, gate_pre, keep],
        [wide_bf16, wide_f32, wide_f32],
        lru_width,
        block_width,
        kernel_flops,
    )
    normed_in_pair = both_rows(normed_in)
    first_keep = keep.reshape(row_count, row_tokens, lru_width)[:, 0]
    head_factor = first_keep * tail_keep.reshape(row_count, row_tokens, lru_width)[:, 0]
    head_grad = first_keep * local_grad.reshape(row_count, row_tokens, lru_width)[:, 0]
    grad_in = carry_before(head_factor, head_grad, True)
    grad_in, gate_pre_low, mixed_pair = tick(
        (grad_in, gate_pre_low, mixed_pair), gate_flight, up_flight
    )
    branch_grad = chip_grad(mixed_pair, middle_half)
    gate_in_grad = chip_grad(normed_in_pair, both_halves(gate_pre_low))
    grad_in, branch_grad, gate_in_grad = lax.optimization_barrier(
        (grad_in, branch_grad, gate_in_grad)
    )
    branch_flight = chip_scatter(branch_grad, "xyz")
    gate_in_flight = chip_scatter(gate_in_grad, "yxz")
    grad_in = launch(grad_in, branch_flight, gate_in_flight)
    square = jax.ShapeDtypeStruct((lru_width, block_width), f32)
    signal_part, head_part, rec_full, input_full, sums = channel_call(
        backward_kernel,
        row_count,
        [
            signal,
            before,
            masks,
            taps,
            rate,
            full_rec,
            full_input,
            conv_low,
            states,
            state_in,
            tail_keep,
            local_grad,
            grad_in,
        ],
        [
            wide_f32,
            jax.ShapeDtypeStruct((row_count * halo, lru_width), f32),
            square,
            square,
            jax.ShapeDtypeStruct((tap_count + 1, lru_width), f32),
        ],
        lru_width,
        block_width,
        3 * kernel_flops // 2,
    )
    signal_part = land(signal_part, gate_flight, up_flight)
    from_right = passed_along(
        head_part.reshape(row_count, halo, lru_width)[:, halo - halo_rows :].astype(bf16),
        "seq",
        -1,
    ).astype(f32)
    signal_low = (
        (
            signal_part.reshape(row_count, row_tokens, lru_width)
            + jnp.pad(from_right, ((0, 0), (row_tokens - halo_rows, 0), (0, 0)))
        )
        .astype(bf16)
        .reshape(token_count, lru_width)
    )
    signal_low = launch(signal_low, gate_flight, up_flight)
    signal_low, gate_pre_low, signal_half = lax.optimization_barrier(
        (signal_low, gate_pre_low, my_half(signal_low))
    )
    gate_part = lax.dot_general(
        gate_pre_low, full_gate_in, transposed, preferred_element_type=f32
    )
    gate_part, sent_half = lax.optimization_barrier(
        (gate_part, swap_cores(other_half(signal_low)))
    )
    signal_grad = chip_grad(
        normed_in_pair, jnp.concatenate([signal_half, sent_half], axis=0)
    )
    pair_grads = jnp.where(core == 0, rec_full, input_full) + swap_cores(
        jnp.where(core == 0, input_full, rec_full).astype(bf16)
    ).astype(f32)
    sizes = [grid_axes()[a][3] for a in "zxyc"]
    chip_count = sizes[0] * sizes[1] * sizes[2]
    quarter = lru_width // 4
    signal_first = chip_scatter(signal_grad[:, :quarter], "xyz")
    pair_rows = pair_grads.astype(bf16).reshape(chip_count, -1, quarter)
    pair_count = pair_rows.shape[1]
    signal_second = chip_scatter(
        jnp.concatenate(
            [signal_grad[:, quarter:].reshape(chip_count, -1, quarter), pair_rows], axis=1
        ).reshape(-1, quarter),
        "yxz",
    )
    signal_low = launch(signal_low, signal_first, signal_second)
    normed_in_grad = gate_part + lax.dot_general(
        signal_low, full_signal, transposed, preferred_element_type=f32
    )
    normed_in_grad = tick(
        after(normed_in_grad, down_shard),
        signal_first,
        signal_second,
        branch_flight,
        gate_in_flight,
    )
    normed_in_grad = land(normed_in_grad, gate_flight, up_flight)
    in_back, gain_in_grad = norm_back(normed_in_grad, inputs, scale_in, gain_in)
    in_back, gain_in_grad = land((in_back, gain_in_grad), signal_first, signal_second)
    signal_last = join_rows([signal_first, signal_second])
    in_back, gain_in_grad = launch((in_back, gain_in_grad), signal_last)
    in_back = land(in_back, branch_flight, gate_in_flight)
    branch_rows = branch_flight.whole.shape[-2]
    branch_flight.whole = branch_flight.whole.reshape(sizes[0], -1, lru_half)
    middle_two = join_rows([branch_flight, gate_in_flight])
    in_back = launch(in_back, middle_two)
    tokens_grad = (middle_grad + in_back).reshape(tokens.shape)

    decay_grad = sums[0] * rate_scale * jax.nn.sigmoid(-decay_full)
    small_grads = [gain_in_grad, gain_mid_grad[0], decay_grad, *(sums[1 + k] for k in range(tap_count))]
    every_small = jnp.concatenate(small_grads)
    for which in "cxyz":
        every_small = every_small + sum(
            hop(every_small, which, d) for d in range(1, grid_axes()[which][3])
        )
    device = lax.axis_index("dp") * lax.axis_size("seq") + lax.axis_index("seq")
    small_shards, start = [], 0
    for grad in small_grads:
        width = grad.shape[0] // device_count
        small_shards.append(
            lax.dynamic_slice_in_dim(every_small, start + device * width, width, 0)
        )
        start += grad.shape[0]
    mlp_gate_shard, mlp_up_shard = [
        jnp.concatenate(pair, axis=1)
        for pair in shards_of([gate_flight.whole, up_flight.whole])
    ]
    branch_pair, gate_in_pair = shards_of(split_rows(middle_two))
    branch_shard = jnp.concatenate(
        [a.reshape(-1, model_width // 2) for a in branch_pair], axis=1
    )
    gate_in_shard = jnp.concatenate(gate_in_pair, axis=1)
    signal_last.parts = [
        signal_last.parts[0],
        signal_last.parts[1] - pair_count,
        pair_count,
    ]
    signal_one, signal_two, pair_halves = shards_of(split_rows(signal_last))
    signal_shard = jnp.concatenate(
        [signal_one[0], signal_two[0], signal_one[1], signal_two[1]], axis=1
    )
    return (
        block_out.reshape(tokens.shape),
        tokens_grad,
        small_shards[0],
        gate_in_shard,
        signal_shard,
        jnp.stack(small_shards[3:]),
        pair_halves[0].reshape(lru_piece, block_width),
        pair_halves[1].reshape(lru_piece, block_width),
        small_shards[2],
        branch_shard,
        small_shards[1],
        mlp_gate_shard,
        mlp_up_shard,
        down_shard.astype(f32),
    )


def solution(mesh):
    rows = P(("dp", "seq"))
    matrix = P(("dp", "seq"), None)
    columns = P(None, ("dp", "seq"))
    tokens = P("dp", "seq", None)
    return jax.shard_map(
        body,
        mesh=mesh,
        in_specs=(
            tokens,
            P("dp", "seq"),
            rows,
            matrix,
            matrix,
            columns,
            matrix,
            matrix,
            rows,
            matrix,
            rows,
            matrix,
            matrix,
            matrix,
            tokens,
        ),
        out_specs=(
            tokens,
            tokens,
            rows,
            matrix,
            matrix,
            columns,
            matrix,
            matrix,
            rows,
            matrix,
            rows,
            matrix,
            matrix,
            matrix,
        ),
        check_vma=False,
    )
```
